256 devices in a mesh: wide: 64 (over x, z_lo, y, core), narrow: 4 (over z_hi).
Axes of the slice: x: 4, y: 4, z: 8 (z_hi: 4, z_lo: 2; z = z_hi * 2 + z_lo), core: 2. Of those that a mesh axis runs over, the one named last changes fastest.
Arguments:
- source_features: bfloat16 [64, 128, 1024], P('wide'), may hold values from -6 to 6
- target_features: bfloat16 [32, 128, 1024], P('narrow', 'wide'), may hold values from -6 to 6
- target_in_taps: float32 [16, 9], replicated, may hold values from -2 to 2
- target_in_bias: float32 [16], replicated, may hold values from -3 to 3
- target_out_taps: float32 [16, 9], replicated, may hold values from -1 to 1
- source_in_taps: float32 [16, 9], replicated, may hold values from -2 to 2
- source_in_bias: float32 [16], replicated, may hold values from -3 to 3
- source_out_taps: float32 [16, 9], replicated, may hold values from -1 to 1
Outputs:
- consensus: bfloat16 [32, 128, 64, 128], P('narrow', 'wide')
The draws below stay inside these ranges and needn't reach their ends.
All inputs are finite; a program needn't handle non-finite values.
Results may differ from the reference program's by a relative error of at most 0.0072.
Values may be sent and summed in bfloat16 or wider, within the bound.
A program may use at most 192 MiB of HBM per device.

```python
import jax
import jax.numpy as jnp
from jax import lax

WA = 128
WB = 128
C = 1024
HIDDEN_SIZE = 16
HA = 64
HB = 32


def centered_taps(key):
    values = jnp.clip(jax.random.normal(key, (HIDDEN_SIZE, 9), jnp.float32), -5.0, 5.0)
    values = values * (9.0 * HIDDEN_SIZE) ** (-0.5)
    return values - jnp.mean(values, axis=1, keepdims=True)


def draw_target_out_taps(key, part):
    return centered_taps(jax.random.fold_in(key, 11))


def draw_source_out_taps(key, part):
    return centered_taps(jax.random.fold_in(key, 23))


def levels(key, shape, shards, low, largest):
    loudness = 1.0
    for position, parts in shards:
        draws = jax.random.uniform(jax.random.fold_in(jax.random.fold_in(key, 6), position), (parts,), jnp.float32, low / len(shards), largest / len(shards))
        loudness = loudness * jnp.repeat(jnp.exp(draws), shape[position] // parts).reshape((-1,) + (1,) * (len(shape) - 1 - position))
    return loudness


def gaussian(own_key, dims, deviation, limit, shards=(), dtype=jnp.bfloat16):
    drawn = jax.random.normal(own_key, dims, jnp.float32) * deviation
    if len(shards) > 0:
        drawn = levels(own_key, dims, shards, -0.22, 0.18) * drawn
    return jnp.clip(drawn, min=-limit, max=limit).astype(dtype)


def setup_inputs(seed: int = 0) -> dict:
    arg_keys = jax.random.split(jax.random.key(seed), 9)
    return {
        "source_features": gaussian(arg_keys[0], (HA, WA, C), 1.0, 6.0, ((0, 64),)),
        "target_features": gaussian(arg_keys[1], (HB, WB, C), 1.0, 6.0, ((0, 4), (1, 64))),
        "target_in_taps": gaussian(arg_keys[2], (HIDDEN_SIZE, 9), 9 ** -0.5, 2.0, (), jnp.float32),
        "target_in_bias": gaussian(arg_keys[3], (HIDDEN_SIZE,), 0.5, 3.0, (), jnp.float32),
        "target_out_taps": draw_target_out_taps(jax.random.fold_in(arg_keys[8], 71), 0),
        "source_in_taps": gaussian(arg_keys[5], (HIDDEN_SIZE, 9), 9 ** -0.5, 2.0, (), jnp.float32),
        "source_in_bias": gaussian(arg_keys[6], (HIDDEN_SIZE,), 0.5, 3.0, (), jnp.float32),
        "source_out_taps": draw_source_out_taps(jax.random.fold_in(arg_keys[8], 71), 0),
    }


def conv_valid(field, weights, first_axis, second_axis):
    size_one = field.shape[first_axis] - 2
    size_two = field.shape[second_axis] - 2
    total = None
    for a in range(3):
        rows = lax.slice_in_dim(field, a, a + size_one, axis=first_axis)
        for b in range(3):
            term = weights[3 * a + b] * lax.slice_in_dim(rows, b, b + size_two, axis=second_axis)
            total = term if total is None else total + term
    return total


def pad_axis(field, axis):
    widths = [(0, 0)] * field.ndim
    widths[axis] = (1, 1)
    return jnp.pad(field, widths)


def consensus_section(field, in_taps, in_bias, out_taps, first_axis, second_axis):
    padded = pad_axis(pad_axis(field.astype(jnp.float32), first_axis), second_axis)
    total = None
    for h in range(in_taps.shape[0]):
        hidden = jnp.maximum(conv_valid(padded, in_taps[h], first_axis, second_axis) + in_bias[h], 0.0)
        hidden = pad_axis(pad_axis(hidden, first_axis), second_axis)
        term = conv_valid(hidden, out_taps[h], first_axis, second_axis)
        total = term if total is None else total + term
    return jnp.maximum(total, 0.0)


def reference(source_features, target_features, target_in_taps, target_in_bias, target_out_taps, source_in_taps, source_in_bias, source_out_taps):
    scale = C ** -0.5
    flat_target = target_features.reshape(HB * WB, C)

    def target_pass(source_row):
        product = jnp.dot(flat_target, source_row.T, preferred_element_type=jnp.float32) * scale
        correlation = product.astype(jnp.bfloat16).reshape(HB, WB, WA)
        sectioned = consensus_section(correlation, target_in_taps, target_in_bias, target_out_taps, 0, 1)
        return sectioned.astype(jnp.bfloat16)

    first = lax.map(target_pass, source_features)
    first = jnp.transpose(first, (1, 2, 0, 3))

    def source_pass(block):
        sectioned = consensus_section(block, source_in_taps, source_in_bias, source_out_taps, 1, 2)
        return sectioned.astype(jnp.bfloat16)

    return lax.map(source_pass, first)
```

```python
import functools

import jax
import jax.numpy as jnp
from jax import lax
from jax.experimental import pallas as pl
from jax.experimental.pallas import tpu as pltpu
from jax.sharding import PartitionSpec as P

F32 = jnp.float32
BF16 = jnp.bfloat16
OFF = -1e38


def split(value):
    high = value.astype(BF16)
    return high, (value - high.astype(F32)).astype(BF16)


def build_target_weights(in_taps_ref, out_taps_ref, w1_hi, w1_lo, w2):
    def chunk(c, carry):
        shape = (256, 256)
        row = lax.broadcasted_iota(jnp.int32, shape, 0)
        cell = (lax.broadcasted_iota(jnp.int32, shape, 1) + c * 256) >> 4
        l_hid = (cell * 205) >> 11
        k_hid = cell - l_hid * 10
        code = ((row >> 4) - l_hid) * 16 + (((row & 15) - k_hid + 2) & 15)
        lanes = pl.ds(pl.multiple_of(c * 256, 256), 256)
        value = jnp.zeros(shape, F32)
        for a in range(3):
            for b in range(3):
                n = 3 * a + b
                taps = in_taps_ref[n : n + 1, :]
                value = jnp.where(code == b * 16 + a, taps, value)
        high, low = split(value)
        w1_hi[:, lanes] = high
        w1_lo[:, lanes] = low

        shape = (16, 1, 128)
        cell = lax.broadcasted_iota(jnp.int32, shape, 0) + c * 16
        lane = lax.broadcasted_iota(jnp.int32, shape, 2)
        l_hid = (cell * 205) >> 11
        k_hid = cell - l_hid * 10
        code = (l_hid - (lane >> 3)) * 16 + ((k_hid - (lane & 7)) & 15)
        code = jnp.broadcast_to(code, (16, 16, 128))
        value = jnp.zeros((16, 16, 128), F32)
        for a in range(3):
            for b in range(3):
                taps = out_taps_ref[3 * a + b]
                value = jnp.where(code == b * 16 + a, taps[None], value)
        high, low = split(value.reshape(256, 128))
        rows = pl.ds(pl.multiple_of(c * 256, 256), 256)
        w2[rows, 0:128] = high
        w2[rows, 128:256] = low
        return carry

    lax.fori_loop(0, 9, chunk, 0)


def target_section(block, x_t, bias_ref, w1_hi, w1_lo, w2, x, bias, acc, out):
    for p in range(11):
        part = x_t[p * 192 : p * 192 + 256, :].astype(F32)
        x[p * 128 : (p + 1) * 128, :] = part.T.astype(BF16)
    shape = (11, 2304)
    patch = lax.broadcasted_iota(jnp.int32, shape, 0)
    cell = lax.broadcasted_iota(jnp.int32, shape, 1) >> 4
    l_hid = (cell * 205) >> 11
    k_at = cell - l_hid * 10 - 1 + block * 8
    l_at = patch * 12 - 1 + l_hid
    valid = (l_at >= 0) & (l_at < 128) & (k_at >= 0) & (k_at < 32) & (cell < 140)
    bias[...] = jnp.where(valid, bias_ref[...], OFF)

    acc[...] = jnp.zeros_like(acc)
    for c in range(9):
        lanes = slice(c * 256, (c + 1) * 256)
        hidden = jnp.dot(x[...], w1_hi[:, lanes], preferred_element_type=F32)
        hidden += jnp.dot(x[...], w1_lo[:, lanes], preferred_element_type=F32)
        hidden = hidden.reshape(11, 128, 256) + bias[:, lanes][:, None, :]
        hidden = jnp.maximum(hidden, 0.0).reshape(1408, 256)
        high, low = split(hidden)
        acc[...] += jnp.dot(high, w2[lanes, :], preferred_element_type=F32)
        acc[:, 0:128] += jnp.dot(low, w2[lanes, 0:128], preferred_element_type=F32)
    for p in range(11):
        rows = slice(p * 128, (p + 1) * 128)
        total = jnp.maximum(acc[rows, 0:128] + acc[rows, 128:256], 0.0).T
        count = 96 if p < 10 else 64
        out[p * 96 : p * 96 + count, :] = total[:count].astype(BF16)


def target_kernel(x_t, in_taps, in_bias, out_taps, out, w1_hi, w1_lo, w2, x, bias, acc):
    build_target_weights(in_taps, out_taps, w1_hi, w1_lo, w2)
    block = lax.axis_index("narrow")
    target_section(block, x_t, in_bias, w1_hi, w1_lo, w2, x, bias, acc, out)


def source_kernel(r_ref, in_taps, in_bias, out_taps, out_ref, w1, w2, x, acc, turned):
    def band(h, carry):
        shape = (128, 128)
        apart = lax.broadcasted_iota(jnp.int32, shape, 0) - lax.broadcasted_iota(
            jnp.int32, shape, 1
        )
        c, at = h // 2, pl.multiple_of((h % 2) * 128, 128)
        for a in range(3):
            for taps, w, first in ((in_taps, w1, True), (out_taps, w2, False)):
                value = jnp.zeros(shape, F32)
                for b in range(3):
                    value = jnp.where(apart == b - 1, taps[h, 3 * a + b], value)
                for n, part in enumerate(split(value)):
                    other = slice((3 * n + a) * 128, (3 * n + a + 1) * 128)
                    if first:
                        w[c, other, pl.ds(at, 128)] = part
                    else:
                        w[c, pl.ds(at, 128), other] = part
        return carry

    lax.fori_loop(0, 16, band, 0)

    zero = jnp.zeros((16, 128), BF16)
    for n in range(2):
        at = n * 384
        x[0:16, at : at + 128] = zero
        x[16:1024, at : at + 128] = r_ref[0:1008, :]
        x[:, at + 128 : at + 256] = r_ref[...]
        x[0:1008, at + 256 : at + 384] = r_ref[16:1024, :]
        x[1008:1024, at + 256 : at + 384] = zero

    acc[...] = jnp.zeros_like(acc)
    for c in range(8):
        hidden = jnp.dot(x[...], w1[c], preferred_element_type=F32)
        hidden = jnp.maximum(hidden + in_bias[:, c * 256 : (c + 1) * 256], 0.0)
        high, low = split(hidden)
        both = jnp.dot(high, w2[c], preferred_element_type=F32)
        rest = jnp.dot(low, w2[c, :, 0:384], preferred_element_type=F32)
        acc[...] += both[:, 0:384] + both[:, 384:768] + rest
    for i in range(64):
        rows = slice(i * 16, (i + 1) * 16)
        total = acc[rows, 128:256]
        if i > 0:
            total += acc[i * 16 - 16 : i * 16, 0:128]
        if i < 63:
            total += acc[i * 16 + 16 : i * 16 + 32, 256:384]
        turned[pl.ds(i, 16, stride=64), :] = jnp.maximum(total, 0.0)
    for k in range(8):
        for l in range(2):
            n = l * 8 + k
            out_ref[k, l] = turned[n * 64 : (n + 1) * 64, :].astype(BF16)


VMEM = pl.BlockSpec(memory_space=pltpu.VMEM)
SMEM = pl.BlockSpec(memory_space=pltpu.SMEM)


def on_device(
    source_features,
    target_features,
    target_in_taps,
    target_in_bias,
    target_out_taps,
    source_in_taps,
    source_in_bias,
    source_out_taps,
):
    scale = source_features.shape[-1] ** (-0.5)
    local = jnp.swapaxes(target_features, 0, 1).reshape(16, 1024)
    flat = lax.all_gather(local, "wide", axis=0, tiled=True)
    product = jnp.dot(flat, source_features[0].T, preferred_element_type=F32) * scale
    cells = product.astype(BF16).reshape(128, 8, 128)
    up = [(i, i + 1) for i in range(3)]
    down = [(i + 1, i) for i in range(3)]
    below = lax.ppermute(cells[:, 6:8], "narrow", up)
    above = lax.ppermute(cells[:, 0:2], "narrow", down)
    gap = jnp.zeros((128, 4, 128), BF16)
    x_t = jnp.concatenate([cells, above, gap, below], axis=1)
    x_t = jnp.pad(x_t, ((2, 6), (0, 0), (0, 0))).reshape(136 * 16, 128)
    section = pl.pallas_call(
        target_kernel,
        out_shape=jax.ShapeDtypeStruct((1024, 128), BF16),
        in_specs=[VMEM] * 4,
        out_specs=VMEM,
        scratch_shapes=[
            pltpu.VMEM((256, 2304), BF16),
            pltpu.VMEM((256, 2304), BF16),
            pltpu.VMEM((2304, 256), BF16),
            pltpu.VMEM((1408, 256), BF16),
            pltpu.VMEM((11, 2304), F32),
            pltpu.VMEM((1408, 256), F32),
        ],
        compiler_params=pltpu.CompilerParams(vmem_limit_bytes=48 * 2**20),
    )(
        x_t,
        jnp.tile(target_in_taps.T, (1, 16)),
        jnp.tile(target_in_bias, 144)[None],
        jnp.broadcast_to(target_out_taps.T[:, :, None], (9, 16, 128)),
    )
    received = lax.all_to_all(
        section.reshape(64, 16, 128), "wide", split_axis=0, concat_axis=0, tiled=True
    )
    return pl.pallas_call(
        source_kernel,
        out_shape=jax.ShapeDtypeStruct((8, 2, 64, 128), BF16),
        in_specs=[VMEM, SMEM, VMEM, SMEM],
        out_specs=VMEM,
        scratch_shapes=[
            pltpu.VMEM((8, 768, 256), BF16),
            pltpu.VMEM((8, 256, 768), BF16),
            pltpu.VMEM((1024, 768), BF16),
            pltpu.VMEM((1024, 384), F32),
            pltpu.VMEM((1024, 128), F32),
        ],
        compiler_params=pltpu.CompilerParams(vmem_limit_bytes=48 * 2**20),
    )(
        received.reshape(1024, 128),
        source_in_taps,
        jnp.repeat(source_in_bias, 128)[None],
        source_out_taps,
    )


def solution(mesh):
    placed = (P("wide", None, None), P("narrow", "wide", None), P(), P(), P(), P(), P(), P())
    return jax.shard_map(
        on_device,
        mesh=mesh,
        in_specs=placed,
        out_specs=P("narrow", "wide", None, None),
        check_vma=False,
    )
```

```python
import functools

import jax
import jax.numpy as jnp
from jax import lax
from jax.experimental import pallas as pl
from jax.experimental.pallas import tpu as pltpu
from jax.sharding import PartitionSpec as P

F32 = jnp.float32
BF16 = jnp.bfloat16
OFF = -1e38


def split(value):
    high = value.astype(BF16)
    return high, (value - high.astype(F32)).astype(BF16)


def build_target_weights(in_taps_ref, out_taps_ref, w1_hi, w1_lo, w2):
    def chunk(c, carry):
        shape = (256, 256)
        row = lax.broadcasted_iota(jnp.int32, shape, 0)
        cell = (lax.broadcasted_iota(jnp.int32, shape, 1) + c * 256) >> 4
        l_hid = (cell * 205) >> 11
        k_hid = cell - l_hid * 10
        code = ((row >> 4) - l_hid) * 16 + (((row & 15) - k_hid + 2) & 15)
        lanes = pl.ds(pl.multiple_of(c * 256, 256), 256)
        value = jnp.zeros(shape, F32)
        for a in range(3):
            for b in range(3):
                n = 3 * a + b
                taps = in_taps_ref[n : n + 1, :]
                value = jnp.where(code == b * 16 + a, taps, value)
        high, low = split(value)
        w1_hi[:, lanes] = high
        w1_lo[:, lanes] = low

        shape = (16, 1, 128)
        cell = lax.broadcasted_iota(jnp.int32, shape, 0) + c * 16
        lane = lax.broadcasted_iota(jnp.int32, shape, 2)
        l_hid = (cell * 205) >> 11
        k_hid = cell - l_hid * 10
        code = (l_hid - (lane >> 3)) * 16 + ((k_hid - (lane & 7)) & 15)
        code = jnp.broadcast_to(code, (16, 16, 128))
        value = jnp.zeros((16, 16, 128), F32)
        for a in range(3):
            for b in range(3):
                taps = out_taps_ref[3 * a + b]
                value = jnp.where(code == b * 16 + a, taps[None], value)
        high, low = split(value.reshape(256, 128))
        rows = pl.ds(pl.multiple_of(c * 256, 256), 256)
        w2[rows, 0:128] = high
        w2[rows, 128:256] = low
        return carry

    lax.fori_loop(0, 9, chunk, 0)


def target_section(block, x_t, bias_ref, w1_hi, w1_lo, w2, x, bias, acc, out):
    for p in range(11):
        part = x_t[p * 192 : p * 192 + 256, :]
        x[p * 128 : (p + 1) * 128, :] = part.T.astype(BF16)
    shape = (11, 2304)
    patch = lax.broadcasted_iota(jnp.int32, shape, 0)
    cell = lax.broadcasted_iota(jnp.int32, shape, 1) >> 4
    l_hid = (cell * 205) >> 11
    k_at = cell - l_hid * 10 - 1 + block * 8
    l_at = patch * 12 - 1 + l_hid
    valid = (l_at >= 0) & (l_at < 128) & (k_at >= 0) & (k_at < 32) & (cell < 140)
    bias[...] = jnp.where(valid, bias_ref[...], OFF)

    acc[...] = jnp.zeros_like(acc)
    for c in range(9):
        lanes = slice(c * 256, (c + 1) * 256)
        hidden = jnp.dot(x[...], w1_hi[:, lanes], preferred_element_type=F32)
        hidden += jnp.dot(x[...], w1_lo[:, lanes], preferred_element_type=F32)
        hidden = hidden.reshape(11, 128, 256) + bias[:, lanes][:, None, :]
        hidden = jnp.maximum(hidden, 0.0).reshape(1408, 256)
        high, low = split(hidden)
        acc[...] += jnp.dot(high, w2[lanes, :], preferred_element_type=F32)
        acc[:, 0:128] += jnp.dot(low, w2[lanes, 0:128], preferred_element_type=F32)
    for p in range(11):
        rows = slice(p * 128, (p + 1) * 128)
        total = jnp.maximum(acc[rows, 0:128] + acc[rows, 128:256], 0.0).T
        count = 96 if p < 10 else 64
        out[p * 96 : p * 96 + count, :] = total[:count].astype(BF16)


def build_source_weights(in_taps, out_taps, w1, w2):
    def band(h, carry):
        shape = (128, 128)
        apart = lax.broadcasted_iota(jnp.int32, shape, 0) - lax.broadcasted_iota(
            jnp.int32, shape, 1
        )
        c, at = h // 2, pl.multiple_of((h % 2) * 128, 128)
        for a in range(3):
            for taps, w, first in ((in_taps, w1, True), (out_taps, w2, False)):
                value = jnp.zeros(shape, F32)
                for b in range(3):
                    value = jnp.where(apart == b - 1, taps[h, 3 * a + b], value)
                for n, part in enumerate(split(value)):
                    other = slice((3 * n + a) * 128, (3 * n + a + 1) * 128)
                    if first:
                        w[c, other, pl.ds(at, 128)] = part
                    else:
                        w[c, pl.ds(at, 128), other] = part
        return carry

    lax.fori_loop(0, 16, band, 0)


def source_section(r_ref, in_bias, out_ref, w1, w2, x, acc, turned):
    zero = jnp.zeros((16, 128), BF16)
    for n in range(2):
        at = n * 384
        x[0:16, at : at + 128] = zero
        x[16:1024, at : at + 128] = r_ref[0:63].reshape(1008, 128)
        x[:, at + 128 : at + 256] = r_ref[...].reshape(1024, 128)
        x[0:1008, at + 256 : at + 384] = r_ref[1:64].reshape(1008, 128)
        x[1008:1024, at + 256 : at + 384] = zero

    acc[...] = jnp.zeros_like(acc)
    for c in range(8):
        hidden = jnp.dot(x[...], w1[c], preferred_element_type=F32)
        hidden = jnp.maximum(hidden + in_bias[:, c * 256 : (c + 1) * 256], 0.0)
        high, low = split(hidden)
        both = jnp.dot(high, w2[c], preferred_element_type=F32)
        rest = jnp.dot(low, w2[c, :, 0:384], preferred_element_type=F32)
        acc[...] += both[:, 0:384] + both[:, 384:768] + rest
    for i in range(64):
        rows = slice(i * 16, (i + 1) * 16)
        total = acc[rows, 128:256]
        if i > 0:
            total += acc[i * 16 - 16 : i * 16, 0:128]
        if i < 63:
            total += acc[i * 16 + 16 : i * 16 + 32, 256:384]
        turned[pl.ds(i, 16, stride=64), :] = jnp.maximum(total, 0.0)
    for k in range(8):
        for l in range(2):
            n = l * 8 + k
            out_ref[k, l] = turned[n * 64 : (n + 1) * 64, :].astype(BF16)


MESH = pl.DeviceIdType.MESH


def push(src, dst, send_sem, recv_sem, device):
    return pltpu.make_async_remote_copy(
        src_ref=src,
        dst_ref=dst,
        send_sem=send_sem,
        recv_sem=recv_sem,
        device_id=device,
        device_id_type=MESH,
    )


class Gather:
    def __init__(self, held, send, recv):
        me = lax.axis_index("wide")
        self.narrow = lax.axis_index("narrow")
        self.held, self.send, self.recv = held, send, recv
        self.core = me % 2
        self.at = (me // 16, (me // 2) % 4)
        self.z = (me // 8) % 2
        self.count = 0
        self.copies = []

    def device(self, x=None, y=None, z=None, core=None):
        x = self.at[0] if x is None else x
        y = self.at[1] if y is None else y
        z = self.z if z is None else z
        core = self.core if core is None else core
        return (((x * 2 + z) * 4 + y) * 2 + core, self.narrow)

    def partners(self):
        found = [self.device(z=1 - self.z), self.device(core=1 - self.core)]
        for axis in "xy":
            for d in range(1, 4):
                found.append(self.along(axis, d))
        return found

    def along(self, axis, d):
        n = (self.at[0 if axis == "x" else 1] + d) % 4
        return self.device(**{axis: n})

    def piece(self, half, back, core=None):
        x, y = ((self.at[n] + 4 - back[n]) % 4 for n in range(2))
        core = self.core if core is None else core
        return self.held.at[x, :, y, core, :, half * 512 : half * 512 + 512]

    def start(self, src, arrives, device):
        n = self.count
        self.count += 1
        copy = push(src, src, self.send.at[n], self.recv.at[n], device)
        copy.start()
        landed = push(src, arrives, self.send.at[n], self.recv.at[n], device)
        self.copies.append((copy, landed))
        return landed

    def first(self):
        x, y = self.at
        slot = self.held.at[x, self.z, y, self.core]
        other = self.held.at[x, 1 - self.z, y, self.core]
        self.pair = self.start(slot, other, self.device(z=1 - self.z))

    def sibling(self, half, back):
        self.siblings.append(
            self.start(
                self.piece(half, back),
                self.piece(half, back, 1 - self.core),
                self.device(core=1 - self.core),
            )
        )

    def second(self):
        self.pair.wait_recv()
        self.siblings = []
        self.early, self.late = {}, {}
        for d in (1, 3, 2):
            for half in range(2):
                axis = "xy"[half]
                back = [0, 0]
                back[half] = d
                landed = self.piece(half, back)
                self.early[half, d] = self.start(
                    self.piece(half, (0, 0)), landed, self.along(axis, d)
                )
        for half in range(2):
            self.spread(half, 0)

    def spread(self, half, e):
        back = [0, 0]
        back[half] = e
        for d in (1, 3, 2):
            from_ = list(back)
            from_[1 - half] = d
            self.late[half, e, d] = self.start(
                self.piece(half, back), self.piece(half, from_), self.along("yx"[half], d)
            )
        self.sibling(half, back)

    def third(self):
        for e in (1, 3, 2):
            for half in range(2):
                self.early[half, e].wait_recv()
                self.spread(half, e)
        for e in (0, 1, 3, 2):
            for d in (1, 3, 2):
                for half in range(2):
                    self.late[half, e, d].wait_recv()
                    back = [0, 0]
                    back[half], back[1 - half] = e, d
                    self.sibling(half, back)

    def finish(self):
        for landed in self.siblings:
            landed.wait_recv()
        for copy, _ in self.copies:
            copy.wait_send()


def whole_kernel(
    t_ref,
    s_ref,
    t_in,
    t_bias,
    t_out,
    s_in,
    s_bias,
    s_out,
    out_ref,
    held,
    x_t,
    w1_hi,
    w1_lo,
    w2,
    x,
    bias,
    acc,
    edge,
    edge_in,
    section,
    received,
    w3,
    w4,
    x4,
    acc4,
    turned,
    g_send,
    g_recv,
    e_send,
    e_recv,
    a_send,
    a_recv,
):
    me = lax.axis_index("wide")
    block = lax.axis_index("narrow")
    gather = Gather(held, g_send, g_recv)
    barrier = pltpu.get_barrier_semaphore()
    above, below = (me, (block + 1) % 4), (me, (block + 3) % 4)
    partners = gather.partners() + [above, below]
    for partner in partners:
        pl.semaphore_signal(barrier, inc=1, device_id=partner, device_id_type=MESH)
    held[gather.at[0], gather.z, gather.at[1], gather.core] = t_ref[...]
    x_t[...] = jnp.zeros_like(x_t)
    pl.semaphore_wait(barrier, len(partners))

    gather.first()
    build_target_weights(t_in, t_out, w1_hi, w1_lo, w2)
    gather.second()
    build_source_weights(s_in, s_out, w3, w4)
    gather.third()
    gather.finish()

    scale = s_ref.shape[-1] ** (-0.5)
    product = lax.dot_general(
        held[...].reshape(1024, 1024),
        s_ref[...],
        (((1,), (1,)), ((), ())),
        preferred_element_type=F32,
    )
    cells = (product * scale).astype(BF16).astype(F32).reshape(128, 8, 128)
    for l in range(128):
        x_t[(l + 2) * 16 : (l + 2) * 16 + 8, :] = cells[l]

    def row(slot):
        return pl.ds(32 + slot, 128, stride=16)

    copies = []
    for n, (device, slots) in enumerate(((above, (6, 7)), (below, (0, 1)))):
        for m, slot in enumerate(slots):
            edge[n, m * 128 : (m + 1) * 128, :] = x_t[row(slot), :].astype(BF16)
        copy = push(edge.at[n], edge_in.at[n], e_send.at[n], e_recv.at[n], device)
        copy.start()
        copies.append(copy)
    for n, (inside, slots) in enumerate(((block > 0, (14, 15)), (block < 3, (8, 9)))):
        copies[n].wait()
        for m, slot in enumerate(slots):
            value = edge_in[n, m * 128 : (m + 1) * 128, :].astype(F32)
            x_t[row(slot), :] = jnp.where(inside, value, 0.0)

    target_section(block, x_t, t_bias, w1_hi, w1_lo, w2, x, bias, acc, section)

    def send(d, carry):
        to = (me + d) % 64
        start = pl.multiple_of(to * 16, 16)
        push(
            section.at[pl.ds(start, 16)], received.at[me], a_send, a_recv, (to, block)
        ).start()
        return carry

    lax.fori_loop(1, 64, send, 0)
    received[me] = section[pl.ds(pl.multiple_of(me * 16, 16), 16)]
    everything = pltpu.make_async_copy(
        received.at[0:63], received.at[0:63], a_recv
    )
    everything.wait()
    source_section(received, s_bias, out_ref, w3, w4, x4, acc4, turned)
    pltpu.make_async_copy(section.at[0:1008], section.at[0:1008], a_send).wait()


VMEM = pl.BlockSpec(memory_space=pltpu.VMEM)
SMEM = pl.BlockSpec(memory_space=pltpu.SMEM)


def on_device(
    source_features,
    target_features,
    target_in_taps,
    target_in_bias,
    target_out_taps,
    source_in_taps,
    source_in_bias,
    source_out_taps,
):
    local = jnp.swapaxes(target_features, 0, 1).reshape(16, 1024)
    return pl.pallas_call(
        whole_kernel,
        out_shape=jax.ShapeDtypeStruct((8, 2, 64, 128), BF16),
        in_specs=[VMEM, VMEM, VMEM, VMEM, VMEM, SMEM, VMEM, SMEM],
        out_specs=VMEM,
        scratch_shapes=[
            pltpu.VMEM((4, 2, 4, 2, 16, 1024), BF16),
            pltpu.VMEM((136 * 16, 128), F32),
            pltpu.VMEM((256, 2304), BF16),
            pltpu.VMEM((256, 2304), BF16),
            pltpu.VMEM((2304, 256), BF16),
            pltpu.VMEM((1408, 256), BF16),
            pltpu.VMEM((11, 2304), F32),
            pltpu.VMEM((1408, 256), F32),
            pltpu.VMEM((2, 256, 128), BF16),
            pltpu.VMEM((2, 256, 128), BF16),
            pltpu.VMEM((1024, 128), BF16),
            pltpu.VMEM((64, 16, 128), BF16),
            pltpu.VMEM((8, 768, 256), BF16),
            pltpu.VMEM((8, 256, 768), BF16),
            pltpu.VMEM((1024, 768), BF16),
            pltpu.VMEM((1024, 384), F32),
            pltpu.VMEM((1024, 128), F32),
            pltpu.SemaphoreType.DMA((63,)),
            pltpu.SemaphoreType.DMA((63,)),
            pltpu.SemaphoreType.DMA((2,)),
            pltpu.SemaphoreType.DMA((2,)),
            pltpu.SemaphoreType.DMA,
            pltpu.SemaphoreType.DMA,
        ],
        compiler_params=pltpu.CompilerParams(
            collective_id=0, has_side_effects=True, vmem_limit_bytes=56 * 2**20
        ),
    )(
        local,
        source_features[0],
        jnp.tile(target_in_taps.T, (1, 16)),
        jnp.tile(target_in_bias, 144)[None],
        jnp.broadcast_to(target_out_taps.T[:, :, None], (9, 16, 128)),
        source_in_taps,
        jnp.repeat(source_in_bias, 128)[None],
        source_out_taps,
    )


def solution(mesh):
    placed = (P("wide", None, None), P("narrow", "wide", None), P(), P(), P(), P(), P(), P())
    return jax.shard_map(
        on_device,
        mesh=mesh,
        in_specs=placed,
        out_specs=P("narrow", "wide", None, None),
        check_vma=False,
    )
```

```python
import functools

import jax
import jax.numpy as jnp
from jax import lax
from jax.experimental import pallas as pl
from jax.experimental.pallas import tpu as pltpu
from jax.sharding import PartitionSpec as P

F32 = jnp.float32
BF16 = jnp.bfloat16
OFF = -1e38


def split(value):
    high = value.astype(BF16)
    return high, (value - high.astype(F32)).astype(BF16)


def spread_taps(t_in, t_bias, t_out, in_rows, out_rows):
    lane = lax.broadcasted_iota(jnp.int32, (1, 256), 1) & 15
    row = lax.broadcasted_iota(jnp.int32, (16, 128), 0)
    for n in range(10):
        value = jnp.zeros((1, 256), F32)
        for h in range(16):
            value = jnp.where(lane == h, t_in[h, n] if n < 9 else t_bias[h], value)
        in_rows[n : n + 1, :] = value
    for n in range(9):
        value = jnp.zeros((16, 128), F32)
        for h in range(16):
            value = jnp.where(row == h, t_out[h, n], value)
        out_rows[n] = value


def build_target_weights(in_taps_ref, out_taps_ref, w1_hi, w1_lo, w2):
    def chunk(c, carry):
        shape = (256, 256)
        row = lax.broadcasted_iota(jnp.int32, shape, 0)
        cell = (lax.broadcasted_iota(jnp.int32, shape, 1) + c * 256) >> 4
        l_hid = (cell * 205) >> 11
        k_hid = cell - l_hid * 10
        code = ((row >> 4) - l_hid) * 16 + (((row & 15) - k_hid + 2) & 15)
        lanes = pl.ds(pl.multiple_of(c * 256, 256), 256)
        value = jnp.zeros(shape, F32)
        for a in range(3):
            for b in range(3):
                n = 3 * a + b
                taps = in_taps_ref[n : n + 1, :]
                value = jnp.where(code == b * 16 + a, taps, value)
        high, low = split(value)
        w1_hi[:, lanes] = high
        w1_lo[:, lanes] = low

        shape = (16, 1, 128)
        cell = lax.broadcasted_iota(jnp.int32, shape, 0) + c * 16
        lane = lax.broadcasted_iota(jnp.int32, shape, 2)
        l_hid = (cell * 205) >> 11
        k_hid = cell - l_hid * 10
        code = (l_hid - (lane >> 3)) * 16 + ((k_hid - (lane & 7)) & 15)
        code = jnp.broadcast_to(code, (16, 16, 128))
        value = jnp.zeros((16, 16, 128), F32)
        for a in range(3):
            for b in range(3):
                taps = out_taps_ref[3 * a + b]
                value = jnp.where(code == b * 16 + a, taps[None], value)
        high, low = split(value.reshape(256, 128))
        rows = pl.ds(pl.multiple_of(c * 256, 256), 256)
        w2[rows, 0:128] = high
        w2[rows, 128:256] = low
        return carry

    lax.fori_loop(0, 9, chunk, 0)


def target_section(block, x_t, bias_ref, w1_hi, w1_lo, w2, x, bias, acc):
    for p in range(11):
        part = x_t[p * 192 : p * 192 + 256, :]
        x[p * 128 : (p + 1) * 128, :] = part.T.astype(BF16)
    shape = (11, 2304)
    patch = lax.broadcasted_iota(jnp.int32, shape, 0)
    cell = lax.broadcasted_iota(jnp.int32, shape, 1) >> 4
    l_hid = (cell * 205) >> 11
    k_at = cell - l_hid * 10 - 1 + block * 8
    l_at = patch * 12 - 1 + l_hid
    valid = (l_at >= 0) & (l_at < 128) & (k_at >= 0) & (k_at < 32) & (cell < 140)
    spread = jnp.concatenate([bias_ref[9:10, :]] * 9, axis=1)
    bias[...] = jnp.where(valid, spread, OFF)

    acc[...] = jnp.zeros_like(acc)
    for c in range(9):
        lanes = slice(c * 256, (c + 1) * 256)
        hidden = jnp.dot(x[...], w1_hi[:, lanes], preferred_element_type=F32)
        hidden += jnp.dot(x[...], w1_lo[:, lanes], preferred_element_type=F32)
        hidden = hidden.reshape(11, 128, 256) + bias[:, lanes][:, None, :]
        hidden = jnp.maximum(hidden, 0.0).reshape(1408, 256)
        high, low = split(hidden)
        acc[...] += jnp.dot(high, w2[lanes, :], preferred_element_type=F32)
        acc[:, 0:128] += jnp.dot(low, w2[lanes, 0:128], preferred_element_type=F32)


def build_source_weights(in_taps, out_taps, w1, w2):
    def band(h, carry):
        shape = (128, 128)
        apart = lax.broadcasted_iota(jnp.int32, shape, 0) - lax.broadcasted_iota(
            jnp.int32, shape, 1
        )
        c, at = h // 2, pl.multiple_of((h % 2) * 128, 128)
        for a in range(3):
            for taps, w, first in ((in_taps, w1, True), (out_taps, w2, False)):
                value = jnp.zeros(shape, F32)
                for b in range(3):
                    value = jnp.where(apart == b - 1, taps[h, 3 * a + b], value)
                for n, part in enumerate(split(value)):
                    other = slice((3 * n + a) * 128, (3 * n + a + 1) * 128)
                    if first:
                        w[c, other, pl.ds(at, 128)] = part
                    else:
                        w[c, pl.ds(at, 128), other] = part
        return carry

    lax.fori_loop(0, 16, band, 0)


def source_section(r_ref, in_bias, out_ref, w1, w2, x, acc, turned):
    zero = jnp.zeros((16, 128), BF16)
    for n in range(2):
        at = n * 384
        x[0:16, at : at + 128] = zero
        x[16:1024, at : at + 128] = r_ref[0:63].reshape(1008, 128)
        x[:, at + 128 : at + 256] = r_ref[...].reshape(1024, 128)
        x[0:1008, at + 256 : at + 384] = r_ref[1:64].reshape(1008, 128)
        x[1008:1024, at + 256 : at + 384] = zero

    acc[...] = jnp.zeros_like(acc)
    lane = lax.broadcasted_iota(jnp.int32, (1, 256), 1)
    for c in range(8):
        hidden = jnp.dot(x[...], w1[c], preferred_element_type=F32)
        hidden = jnp.maximum(hidden + jnp.where(lane < 128, in_bias[2 * c], in_bias[2 * c + 1]), 0.0)
        high, low = split(hidden)
        both = jnp.dot(high, w2[c], preferred_element_type=F32)
        rest = jnp.dot(low, w2[c, :, 0:384], preferred_element_type=F32)
        acc[...] += both[:, 0:384] + both[:, 384:768] + rest
    for i in range(64):
        rows = slice(i * 16, (i + 1) * 16)
        total = acc[rows, 128:256]
        if i > 0:
            total += acc[i * 16 - 16 : i * 16, 0:128]
        if i < 63:
            total += acc[i * 16 + 16 : i * 16 + 32, 256:384]
        turned[pl.ds(i, 16, stride=64), :] = jnp.maximum(total, 0.0)
    for k in range(8):
        for l in range(2):
            n = l * 8 + k
            out_ref[k, l] = turned[n * 64 : (n + 1) * 64, :].astype(BF16)


MESH = pl.DeviceIdType.MESH


def push(src, dst, send_sem, recv_sem, device):
    return pltpu.make_async_remote_copy(
        src_ref=src,
        dst_ref=dst,
        send_sem=send_sem,
        recv_sem=recv_sem,
        device_id=device,
        device_id_type=MESH,
    )


class Gather:
    def __init__(self, held, send, recv):
        me = lax.axis_index("wide")
        self.narrow = lax.axis_index("narrow")
        self.held, self.send, self.recv = held, send, recv
        self.core = me % 2
        self.at = (me // 16, (me // 2) % 4)
        self.z = (me // 8) % 2
        self.count = 0
        self.copies = []

    def device(self, x=None, y=None, z=None, core=None, narrow=None):
        x = self.at[0] if x is None else x
        y = self.at[1] if y is None else y
        z = self.z if z is None else z
        core = self.core if core is None else core
        narrow = self.narrow if narrow is None else narrow
        return (((x * 2 + z) * 4 + y) * 2 + core, narrow)

    def along(self, half, d, other=0):
        n = (self.at[half] + d) % 4
        return self.device(z=(self.z + other) % 2, **{"xy"[half]: n})

    def partners(self):
        found = [self.device(core=1 - self.core)]
        for d, other in self.near():
            for half in range(2):
                if d > 0 or half == 0:
                    found.append(self.along(half, d, other))
        for step in (1, 3):
            for core in (self.core, 1 - self.core):
                found.append(self.device(core=core, narrow=(self.narrow + step) % 4))
        return found

    def near(self):
        return [(0, 1)] + [(d, other) for other in (0, 1) for d in (1, 3, 2)]

    def start(self, src, arrives, device):
        n = self.count
        self.count += 1
        copy = push(src, src, self.send.at[n], self.recv.at[n], device)
        copy.start()
        self.copies.append(copy)
        return push(src, arrives, self.send.at[n], self.recv.at[n], device)

    def back(self, half, steps):
        at = list(self.at)
        at[half] = (at[half] + 4 - steps) % 4
        return at

    def first(self):
        self.early, self.late = {}, {}
        for d, other in self.near():
            for half in range(2):
                lanes = slice(half * 512, half * 512 + 512)
                x, y = self.at
                src = self.held.at[x, self.z, y, :, lanes]
                x, y = self.back(half, d)
                landed = self.held.at[x, (self.z + other) % 2, y, :, lanes]
                self.early[half, d, other] = self.start(
                    src, landed, self.along(half, d, other)
                )

    def second(self):
        for e in (0, 1, 3, 2):
            for half in range(2):
                lanes = slice(half * 512, half * 512 + 512)
                for other in range(2):
                    if (e, other) != (0, 0):
                        self.early[half, e, other].wait_recv()
                at = self.back(half, e)
                x, y = at
                src = self.held.at[x, :, y, :, lanes]
                for d in (1, 3, 2):
                    x, y = at
                    if half == 0:
                        y = (y + 4 - d) % 4
                    else:
                        x = (x + 4 - d) % 4
                    landed = self.held.at[x, :, y, :, lanes]
                    self.late[half, e, d] = self.start(
                        src, landed, self.along(1 - half, d)
                    )

    def finish(self):
        for landed in self.late.values():
            landed.wait_recv()
        for copy in self.copies:
            copy.wait_send()


def whole_kernel(
    t_ref,
    s_ref,
    t_in,
    t_bias,
    t_out,
    s_in,
    s_bias,
    s_out,
    out_ref,
    held,
    x_t,
    w1_hi,
    w1_lo,
    w2,
    x,
    bias,
    acc,
    s_all,
    cells_f,
    cells_out,
    cells_in,
    edge,
    edge_in,
    section,
    received,
    w3,
    w4,
    x4,
    acc4,
    turned,
    in_rows,
    out_rows,
    g_send,
    g_recv,
    e_send,
    e_recv,
    a_send,
    a_recv,
):
    me = lax.axis_index("wide")
    block = lax.axis_index("narrow")
    gather = Gather(held, g_send, g_recv)
    core = gather.core
    barrier = pltpu.get_barrier_semaphore()
    partners = gather.partners()
    for partner in partners:
        pl.semaphore_signal(barrier, inc=1, device_id=partner, device_id_type=MESH)
    mine = t_ref[...].astype(F32)
    mine = jnp.concatenate([mine[:, 0, :], mine[:, 1, :]], axis=0)
    held[gather.at[0], gather.z, gather.at[1]] = mine.astype(BF16)
    s_all[0:128, :] = s_ref[...]
    x_t[...] = jnp.zeros_like(x_t)
    pl.semaphore_wait(barrier, len(partners))

    sibling = gather.device(core=1 - core)
    gather.first()
    other_row = push(s_ref, s_all.at[128:256], e_send.at[5], e_recv.at[5], sibling)
    other_row.start()
    spread_taps(t_in, t_bias, t_out, in_rows, out_rows)
    build_target_weights(in_rows, out_rows, w1_hi, w1_lo, w2)
    gather.second()
    build_source_weights(s_in, s_out, w3, w4)
    other_row.wait()
    gather.finish()

    scale = s_ref.shape[-1] ** (-0.5)
    product = lax.dot_general(
        held[...].reshape(512, 1024),
        s_all[...],
        (((1,), (1,)), ((), ())),
        preferred_element_type=F32,
    )
    product = (product * scale).astype(BF16)
    cells_f[0] = product[:, 0:128].astype(F32)
    cells_f[1] = product[:, 128:256].astype(F32)
    cells_out[...] = product[:, 128:256]
    copies = []
    n = 4
    copies.append(push(cells_out, cells_in, e_send.at[n], e_recv.at[n], sibling))
    copies[0].start()
    for up, slots in enumerate(((0, 1), (6, 7))):
        for away in range(2):
            n = up * 2 + away
            for m, slot in enumerate(slots):
                rows = cells_f[away, pl.ds(slot, 64, stride=8), :]
                edge[n, m * 64 : (m + 1) * 64, :] = rows.astype(BF16)
            device = gather.device(
                core=(core + away) % 2, narrow=(block + (1 if up else 3)) % 4
            )
            copy = push(edge.at[n], edge_in.at[n], e_send.at[n], e_recv.at[n], device)
            copy.start()
            copies.append(copy)

    def place(cells, core):
        for n in range(64):
            first = pl.multiple_of(32 + core * 32 + (n // 2) * 64 + (n % 2) * 16, 8)
            x_t[pl.ds(first, 8), :] = cells[n * 8 : n * 8 + 8]

    place(cells_f[0], core)
    for copy in copies:
        copy.wait()
    place(cells_in[...].astype(F32), 1 - core)
    for up, (inside, slots) in enumerate(((block < 3, (8, 9)), (block > 0, (14, 15)))):
        for away in range(2):
            at = (core + away) % 2
            for m, slot in enumerate(slots):
                value = edge_in[up * 2 + away, m * 64 : (m + 1) * 64, :].astype(F32)
                value = jnp.where(inside, value, 0.0)
                cells_f[away, 0:64, :] = value
                for l in range(2):
                    x_t[pl.ds(32 + at * 32 + l * 16 + slot, 32, stride=64), :] = cells_f[
                        away, pl.ds(l, 32, stride=2), :
                    ]

    target_section(block, x_t, in_rows, w1_hi, w1_lo, w2, x, bias, acc)

    def send(step, carry):
        p = (me // 6 + step) % 11
        rows = pl.ds(pl.multiple_of(p * 128, 128), 128)
        total = jnp.maximum(acc[rows, 0:128] + acc[rows, 128:256], 0.0).T
        section[pl.ds(pl.multiple_of(p * 96, 32), 96), :] = total[:96].astype(BF16)
        for q in range(6):
            to = p * 6 + q

            @pl.when((to < 64) & (to != me))
            def _():
                src = section.at[pl.ds(pl.multiple_of(to * 16, 16), 16)]
                push(src, received.at[me], a_send, a_recv, (to, block)).start()

        return carry

    lax.fori_loop(0, 11, send, 0)
    received[me] = section[pl.ds(pl.multiple_of(me * 16, 16), 16)]
    everything = pltpu.make_async_copy(
        received.at[0:63], received.at[0:63], a_recv
    )
    everything.wait()
    source_section(received, s_bias, out_ref, w3, w4, x4, acc4, turned)
    pltpu.make_async_copy(section.at[0:1008], section.at[0:1008], a_send).wait()


VMEM = pl.BlockSpec(memory_space=pltpu.VMEM)
SMEM = pl.BlockSpec(memory_space=pltpu.SMEM)


def on_device(
    source_features,
    target_features,
    target_in_taps,
    target_in_bias,
    target_out_taps,
    source_in_taps,
    source_in_bias,
    source_out_taps,
):
    return pl.pallas_call(
        whole_kernel,
        out_shape=jax.ShapeDtypeStruct((8, 2, 64, 128), BF16),
        in_specs=[VMEM, VMEM] + [SMEM] * 6,
        out_specs=VMEM,
        scratch_shapes=[
            pltpu.VMEM((4, 2, 4, 16, 1024), BF16),
            pltpu.VMEM((136 * 16, 128), F32),
            pltpu.VMEM((256, 2304), BF16),
            pltpu.VMEM((256, 2304), BF16),
            pltpu.VMEM((2304, 256), BF16),
            pltpu.VMEM((1408, 256), BF16),
            pltpu.VMEM((11, 2304), F32),
            pltpu.VMEM((1408, 256), F32),
            pltpu.VMEM((256, 1024), BF16),
            pltpu.VMEM((2, 512, 128), F32),
            pltpu.VMEM((512, 128), BF16),
            pltpu.VMEM((512, 128), BF16),
            pltpu.VMEM((4, 128, 128), BF16),
            pltpu.VMEM((4, 128, 128), BF16),
            pltpu.VMEM((1056, 128), BF16),
            pltpu.VMEM((64, 16, 128), BF16),
            pltpu.VMEM((8, 768, 256), BF16),
            pltpu.VMEM((8, 256, 768), BF16),
            pltpu.VMEM((1024, 768), BF16),
            pltpu.VMEM((1024, 384), F32),
            pltpu.VMEM((1024, 128), F32),
            pltpu.VMEM((16, 256), F32),
            pltpu.VMEM((9, 16, 128), F32),
            pltpu.SemaphoreType.DMA((38,)),
            pltpu.SemaphoreType.DMA((38,)),
            pltpu.SemaphoreType.DMA((6,)),
            pltpu.SemaphoreType.DMA((6,)),
            pltpu.SemaphoreType.DMA,
            pltpu.SemaphoreType.DMA,
        ],
        compiler_params=pltpu.CompilerParams(
            collective_id=0, has_side_effects=True, vmem_limit_bytes=56 * 2**20
        ),
    )(
        target_features,
        source_features[0],
        target_in_taps,
        target_in_bias,
        target_out_taps,
        source_in_taps,
        source_in_bias,
        source_out_taps,
    )


def solution(mesh):
    placed = (P("wide", None, None), P("narrow", "wide", None), P(), P(), P(), P(), P(), P())
    return jax.shard_map(
        on_device,
        mesh=mesh,
        in_specs=placed,
        out_specs=P("narrow", "wide", None, None),
        check_vma=False,
    )
```

```python
import functools

import jax
import jax.numpy as jnp
from jax import lax
from jax.experimental import pallas as pl
from jax.experimental.pallas import tpu as pltpu
from jax.sharding import PartitionSpec as P

F32 = jnp.float32
BF16 = jnp.bfloat16
OFF = -1e38


def split(value):
    high = value.astype(BF16)
    return high, (value - high.astype(F32)).astype(BF16)


def spread_taps(t_in, t_bias, t_out, in_rows, out_rows):
    lane = lax.broadcasted_iota(jnp.int32, (1, 256), 1) & 15
    row = lax.broadcasted_iota(jnp.int32, (16, 128), 0)
    for n in range(10):
        value = jnp.zeros((1, 256), F32)
        for h in range(16):
            value = jnp.where(lane == h, t_in[h, n] if n < 9 else t_bias[h], value)
        in_rows[n : n + 1, :] = value
    for n in range(9):
        value = jnp.zeros((16, 128), F32)
        for h in range(16):
            value = jnp.where(row == h, t_out[h, n], value)
        out_rows[n] = value


def place_of(cell):
    inner = (cell * 171) >> 10
    rest = cell - 84
    l_edge, k_edge = rest >> 2, rest & 3
    l_hid = jnp.where(cell < 84, inner, l_edge)
    k_hid = jnp.where(cell < 84, cell - inner * 6 + 2, jnp.where(k_edge < 2, k_edge, k_edge + 6))
    return l_hid, k_hid


def chosen(code, taps):
    value = jnp.zeros(code.shape, F32)
    for a in range(3):
        for b in range(3):
            value = jnp.where(code == b * 16 + a, taps(3 * a + b), value)
    return value


def build_target_weights(in_taps_ref, out_taps_ref, w1, wh, w2):
    def taps_in(n):
        return in_taps_ref[n : n + 1, :]

    def chunk(c, carry):
        shape = (128, 256)
        row = lax.broadcasted_iota(jnp.int32, shape, 0)
        cell = (lax.broadcasted_iota(jnp.int32, (1, 256), 1) + c * 256) >> 4
        l_hid, k_hid = place_of(cell)
        code = ((row >> 3) - l_hid) * 16 + (((row & 7) - k_hid + 2) & 15)
        lanes = pl.ds(pl.multiple_of(c * 256, 256), 256)
        high, low = split(chosen(code, taps_in))
        w1[0:128, lanes] = high
        w1[128:256, lanes] = low

        cell = lax.broadcasted_iota(jnp.int32, (16, 1, 128), 0) + c * 16
        lane = lax.broadcasted_iota(jnp.int32, (16, 1, 128), 2)
        l_hid, k_hid = place_of(cell)
        code = (l_hid - (lane >> 3)) * 16 + ((k_hid - (lane & 7)) & 15)
        code = jnp.broadcast_to(code, (16, 16, 128))
        high, low = split(chosen(code, lambda n: out_taps_ref[n][None]).reshape(256, 128))
        rows = pl.ds(pl.multiple_of(c * 256, 256), 256)
        w2[rows, 0:128] = high
        w2[rows, 128:256] = low
        return carry

    lax.fori_loop(0, 9, chunk, 0)

    def edge_chunk(c, carry):
        row = lax.broadcasted_iota(jnp.int32, (64, 256), 0)
        cell = (lax.broadcasted_iota(jnp.int32, (1, 256), 1) + c * 256 + 1280) >> 4
        l_hid, k_hid = place_of(cell)
        m = row & 3
        k_in = jnp.where(m < 2, m - 2, m + 6)
        code = ((row >> 2) - l_hid) * 16 + ((k_in - k_hid + 2) & 15)
        lanes = pl.ds(pl.multiple_of(c * 256, 256), 256)
        high, low = split(chosen(code, taps_in))
        wh[0:64, lanes] = high
        wh[64:128, lanes] = low
        return carry

    lax.fori_loop(0, 4, edge_chunk, 0)


def target_bias(block, first, spread_ref, bias):
    shape = (11, 2304)
    patch = lax.broadcasted_iota(jnp.int32, shape, 0) + first
    patch = jnp.where(patch >= 11, patch - 11, patch)
    cell = lax.broadcasted_iota(jnp.int32, (1, 2304), 1) >> 4
    l_hid, k_hid = place_of(cell)
    k_at = k_hid - 1 + block * 8
    l_at = patch * 12 - 1 + l_hid
    valid = (l_at >= 0) & (l_at < 128) & (k_at >= 0) & (k_at < 32) & (cell < 140)
    spread = jnp.concatenate([spread_ref[9:10, :]] * 9, axis=1)
    bias[...] = jnp.where(valid, spread, OFF)


def target_chunk(c, steps, x, xh, bias, w1, wh, w2, acc):
    rows = slice(steps.start * 128, steps.stop * 128)
    count = steps.stop - steps.start
    lanes = slice(c * 256, (c + 1) * 256)
    hidden = jnp.dot(x[rows, :], w1[:, lanes], preferred_element_type=F32)
    if c >= 5:
        edge_lanes = slice(c * 256 - 1280, c * 256 - 1024)
        hidden += jnp.dot(xh[rows, :], wh[:, edge_lanes], preferred_element_type=F32)
    hidden = hidden.reshape(count, 128, 256) + bias[steps, lanes][:, None, :]
    high, low = split(jnp.maximum(hidden, 0.0).reshape(count * 128, 256))
    first = jnp.dot(high, w2[lanes, :], preferred_element_type=F32)
    rest = jnp.dot(low, w2[lanes, 0:128], preferred_element_type=F32)
    if c == 0:
        acc[rows, :] = first
    else:
        acc[rows, :] += first
    acc[rows, 0:128] += rest


def build_source_weights(in_taps, out_taps, w1, w2):
    def band(h, carry):
        shape = (128, 128)
        apart = lax.broadcasted_iota(jnp.int32, shape, 0) - lax.broadcasted_iota(
            jnp.int32, shape, 1
        )
        c, at = h // 2, pl.multiple_of((h % 2) * 128, 128)
        for a in range(3):
            for taps, w, first in ((in_taps, w1, True), (out_taps, w2, False)):
                value = jnp.zeros(shape, F32)
                for b in range(3):
                    value = jnp.where(apart == b - 1, taps[h, 3 * a + b], value)
                for n, part in enumerate(split(value)):
                    other = slice((3 * n + a) * 128, (3 * n + a + 1) * 128)
                    if first:
                        w[c, other, pl.ds(at, 128)] = part
                    else:
                        w[c, pl.ds(at, 128), other] = part
        return carry

    lax.fori_loop(0, 16, band, 0)


def source_section(r_ref, in_bias, out_ref, w1, w2, x, acc, turned):
    zero = jnp.zeros((16, 128), BF16)
    for n in range(2):
        at = n * 384
        x[0:16, at : at + 128] = zero
        x[16:1024, at : at + 128] = r_ref[0:63].reshape(1008, 128)
        x[:, at + 128 : at + 256] = r_ref[...].reshape(1024, 128)
        x[0:1008, at + 256 : at + 384] = r_ref[1:64].reshape(1008, 128)
        x[1008:1024, at + 256 : at + 384] = zero

    acc[...] = jnp.zeros_like(acc)
    lane = lax.broadcasted_iota(jnp.int32, (1, 256), 1)
    for c in range(8):
        hidden = jnp.dot(x[...], w1[c], preferred_element_type=F32)
        hidden = jnp.maximum(hidden + jnp.where(lane < 128, in_bias[2 * c], in_bias[2 * c + 1]), 0.0)
        high, low = split(hidden)
        both = jnp.dot(high, w2[c], preferred_element_type=F32)
        rest = jnp.dot(low, w2[c, :, 0:384], preferred_element_type=F32)
        acc[...] += both[:, 0:384] + both[:, 384:768] + rest
    for i in range(64):
        rows = slice(i * 16, (i + 1) * 16)
        total = acc[rows, 128:256]
        if i > 0:
            total += acc[i * 16 - 16 : i * 16, 0:128]
        if i < 63:
            total += acc[i * 16 + 16 : i * 16 + 32, 256:384]
        turned[pl.ds(i, 16, stride=64), :] = jnp.maximum(total, 0.0)
    for k in range(8):
        for l in range(2):
            n = l * 8 + k
            out_ref[k, l] = turned[n * 64 : (n + 1) * 64, :].astype(BF16)


MESH = pl.DeviceIdType.MESH


def push(src, dst, send_sem, recv_sem, device):
    return pltpu.make_async_remote_copy(
        src_ref=src,
        dst_ref=dst,
        send_sem=send_sem,
        recv_sem=recv_sem,
        device_id=device,
        device_id_type=MESH,
    )


class Gather:
    def __init__(self, held, send, recv):
        me = lax.axis_index("wide")
        self.narrow = lax.axis_index("narrow")
        self.held, self.send, self.recv = held, send, recv
        self.core = me % 2
        self.at = (me // 16, (me // 2) % 4)
        self.z = (me // 8) % 2
        self.count = 0
        self.copies = []

    def device(self, x=None, y=None, z=None, core=None, narrow=None):
        x = self.at[0] if x is None else x
        y = self.at[1] if y is None else y
        z = self.z if z is None else z
        core = self.core if core is None else core
        narrow = self.narrow if narrow is None else narrow
        return (((x * 2 + z) * 4 + y) * 2 + core, narrow)

    def along(self, half, d, other=0):
        n = (self.at[half] + d) % 4
        return self.device(z=(self.z + other) % 2, **{"xy"[half]: n})

    def partners(self):
        found = [self.device(core=1 - self.core)]
        for d, other in self.near():
            for half in range(2):
                if d > 0 or half == 0:
                    found.append(self.along(half, d, other))
        for step in (1, 3):
            for core in (self.core, 1 - self.core):
                found.append(self.device(core=core, narrow=(self.narrow + step) % 4))
        return found

    def near(self):
        return [(0, 1)] + [(d, other) for other in (0, 1) for d in (1, 3, 2)]

    def start(self, src, arrives, device):
        n = self.count
        self.count += 1
        copy = push(src, src, self.send.at[n], self.recv.at[n], device)
        copy.start()
        self.copies.append(copy)
        return push(src, arrives, self.send.at[n], self.recv.at[n], device)

    def back(self, half, steps):
        at = list(self.at)
        at[half] = (at[half] + 4 - steps) % 4
        return at

    def first(self):
        self.early, self.late = {}, {}
        for d, other in self.near():
            for half in range(2):
                lanes = slice(half * 512, half * 512 + 512)
                x, y = self.at
                src = self.held.at[x, self.z, y, :, lanes]
                x, y = self.back(half, d)
                landed = self.held.at[x, (self.z + other) % 2, y, :, lanes]
                self.early[half, d, other] = self.start(
                    src, landed, self.along(half, d, other)
                )

    def second(self):
        for e in (0, 1, 3, 2):
            for half in range(2):
                lanes = slice(half * 512, half * 512 + 512)
                for other in range(2):
                    if (e, other) != (0, 0):
                        self.early[half, e, other].wait_recv()
                at = self.back(half, e)
                x, y = at
                src = self.held.at[x, :, y, :, lanes]
                for d in (1, 3, 2):
                    x, y = at
                    if half == 0:
                        y = (y + 4 - d) % 4
                    else:
                        x = (x + 4 - d) % 4
                    landed = self.held.at[x, :, y, :, lanes]
                    self.late[half, e, d] = self.start(
                        src, landed, self.along(1 - half, d)
                    )

    def finish(self):
        for landed in self.late.values():
            landed.wait_recv()
        for copy in self.copies:
            copy.wait_send()


def whole_kernel(
    t_ref,
    s_ref,
    t_in,
    t_bias,
    t_out,
    s_in,
    s_bias,
    s_out,
    out_ref,
    held,
    x_t,
    xh_t,
    w1,
    wh,
    w2,
    x,
    xh,
    bias,
    acc,
    s_all,
    cells_f,
    cells_out,
    cells_in,
    edge,
    edge_in,
    section,
    received,
    w3,
    w4,
    x4,
    acc4,
    turned,
    in_rows,
    out_rows,
    g_send,
    g_recv,
    e_send,
    e_recv,
    a_send,
    a_recv,
):
    me = lax.axis_index("wide")
    block = lax.axis_index("narrow")
    gather = Gather(held, g_send, g_recv)
    core = gather.core
    barrier = pltpu.get_barrier_semaphore()
    partners = gather.partners()
    for partner in partners:
        pl.semaphore_signal(barrier, inc=1, device_id=partner, device_id_type=MESH)
    mine = t_ref[...].astype(F32)
    mine = jnp.concatenate([mine[:, 0, :], mine[:, 1, :]], axis=0)
    held[gather.at[0], gather.z, gather.at[1]] = mine.astype(BF16)
    s_all[0:128, :] = s_ref[...]
    x_t[...] = jnp.zeros_like(x_t)
    xh_t[...] = jnp.zeros_like(xh_t)
    pl.semaphore_wait(barrier, len(partners))

    sibling = gather.device(core=1 - core)
    gather.first()
    other_row = push(s_ref, s_all.at[128:256], e_send.at[5], e_recv.at[5], sibling)
    other_row.start()
    spread_taps(t_in, t_bias, t_out, in_rows, out_rows)
    build_target_weights(in_rows, out_rows, w1, wh, w2)
    target_bias(block, me // 6, in_rows, bias)
    gather.second()
    build_source_weights(s_in, s_out, w3, w4)
    other_row.wait()
    gather.finish()

    scale = s_ref.shape[-1] ** (-0.5)
    product = lax.dot_general(
        held[...].reshape(512, 1024),
        s_all[...],
        (((1,), (1,)), ((), ())),
        preferred_element_type=F32,
    )
    product = (product * scale).astype(BF16)
    cells_f[0] = product[:, 0:128].astype(F32)
    cells_f[1] = product[:, 128:256].astype(F32)
    cells_out[...] = product[:, 128:256]
    copies = []
    n = 4
    copies.append(push(cells_out, cells_in, e_send.at[n], e_recv.at[n], sibling))
    copies[0].start()
    for up, slots in enumerate(((0, 1), (6, 7))):
        for away in range(2):
            n = up * 2 + away
            for m, slot in enumerate(slots):
                rows = cells_f[away, pl.ds(slot, 64, stride=8), :]
                edge[n, m * 64 : (m + 1) * 64, :] = rows.astype(BF16)
            device = gather.device(
                core=(core + away) % 2, narrow=(block + (1 if up else 3)) % 4
            )
            copy = push(edge.at[n], edge_in.at[n], e_send.at[n], e_recv.at[n], device)
            copy.start()
            copies.append(copy)

    def place(cells, core):
        for n in range(64):
            first = pl.multiple_of(16 + core * 16 + (n // 2) * 32 + (n % 2) * 8, 8)
            x_t[pl.ds(first, 8), :] = cells[n * 8 : n * 8 + 8]

    patches = [(me // 6 + step) % 11 for step in range(11)]
    place(cells_f[0], core)
    copies[0].wait()
    place(cells_in[...].astype(F32), 1 - core)
    for step, p in enumerate(patches):
        turned_part = x_t[pl.ds(pl.multiple_of(p * 96, 32), 128), :].T.astype(BF16)
        x[step * 128 : step * 128 + 128, 0:128] = turned_part
        x[step * 128 : step * 128 + 128, 128:256] = turned_part

    every = slice(0, 11)
    for c in range(5):
        target_chunk(c, every, x, xh, bias, w1, wh, w2, acc)

    for copy in copies[1:]:
        copy.wait()
    for up, (inside, slots) in enumerate(((block < 3, (2, 3)), (block > 0, (0, 1)))):
        for away in range(2):
            at = (core + away) % 2
            for m, slot in enumerate(slots):
                value = edge_in[up * 2 + away, m * 64 : (m + 1) * 64, :].astype(F32)
                value = jnp.where(inside, value, 0.0)
                cells_f[away, 0:64, :] = value
                for l in range(2):
                    xh_t[pl.ds(8 + at * 8 + l * 4 + slot, 32, stride=16), :] = cells_f[
                        away, pl.ds(l, 32, stride=2), :
                    ]
    for step, p in enumerate(patches):
        turned_part = xh_t[pl.ds(pl.multiple_of(p * 48, 16), 64), :].T.astype(BF16)
        xh[step * 128 : step * 128 + 128, :] = jnp.concatenate(
            [turned_part, turned_part], axis=1
        )

    for steps in (slice(0, 6), slice(6, 11)):
        for c in range(5, 9):
            target_chunk(c, steps, x, xh, bias, w1, wh, w2, acc)
        for step in range(steps.start, steps.stop):
            p = patches[step]
            rows = slice(step * 128, step * 128 + 128)
            total = jnp.maximum(acc[rows, 0:128] + acc[rows, 128:256], 0.0).T
            section[pl.ds(pl.multiple_of(p * 96, 32), 96), :] = total[:96].astype(BF16)
        for step in range(steps.start, steps.stop):
            for q in range(6):
                to = patches[step] * 6 + q

                @pl.when((to < 64) & (to != me))
                def _():
                    src = section.at[pl.ds(pl.multiple_of(to * 16, 16), 16)]
                    push(src, received.at[me], a_send, a_recv, (to, block)).start()

    received[me] = section[pl.ds(pl.multiple_of(me * 16, 16), 16)]
    everything = pltpu.make_async_copy(
        received.at[0:63], received.at[0:63], a_recv
    )
    everything.wait()
    source_section(received, s_bias, out_ref, w3, w4, x4, acc4, turned)
    pltpu.make_async_copy(section.at[0:1008], section.at[0:1008], a_send).wait()


VMEM = pl.BlockSpec(memory_space=pltpu.VMEM)
SMEM = pl.BlockSpec(memory_space=pltpu.SMEM)


def on_device(
    source_features,
    target_features,
    target_in_taps,
    target_in_bias,
    target_out_taps,
    source_in_taps,
    source_in_bias,
    source_out_taps,
):
    return pl.pallas_call(
        whole_kernel,
        out_shape=jax.ShapeDtypeStruct((8, 2, 64, 128), BF16),
        in_specs=[VMEM, VMEM] + [SMEM] * 6,
        out_specs=VMEM,
        scratch_shapes=[
            pltpu.VMEM((4, 2, 4, 16, 1024), BF16),
            pltpu.VMEM((136 * 8, 128), F32),
            pltpu.VMEM((136 * 4, 128), F32),
            pltpu.VMEM((256, 2304), BF16),
            pltpu.VMEM((128, 1024), BF16),
            pltpu.VMEM((2304, 256), BF16),
            pltpu.VMEM((1408, 256), BF16),
            pltpu.VMEM((1408, 128), BF16),
            pltpu.VMEM((11, 2304), F32),
            pltpu.VMEM((1408, 256), F32),
            pltpu.VMEM((256, 1024), BF16),
            pltpu.VMEM((2, 512, 128), F32),
            pltpu.VMEM((512, 128), BF16),
            pltpu.VMEM((512, 128), BF16),
            pltpu.VMEM((4, 128, 128), BF16),
            pltpu.VMEM((4, 128, 128), BF16),
            pltpu.VMEM((1056, 128), BF16),
            pltpu.VMEM((64, 16, 128), BF16),
            pltpu.VMEM((8, 768, 256), BF16),
            pltpu.VMEM((8, 256, 768), BF16),
            pltpu.VMEM((1024, 768), BF16),
            pltpu.VMEM((1024, 384), F32),
            pltpu.VMEM((1024, 128), F32),
            pltpu.VMEM((16, 256), F32),
            pltpu.VMEM((9, 16, 128), F32),
            pltpu.SemaphoreType.DMA((38,)),
            pltpu.SemaphoreType.DMA((38,)),
            pltpu.SemaphoreType.DMA((6,)),
            pltpu.SemaphoreType.DMA((6,)),
            pltpu.SemaphoreType.DMA,
            pltpu.SemaphoreType.DMA,
        ],
        compiler_params=pltpu.CompilerParams(
            collective_id=0, has_side_effects=True, vmem_limit_bytes=56 * 2**20
        ),
    )(
        target_features,
        source_features[0],
        target_in_taps,
        target_in_bias,
        target_out_taps,
        source_in_taps,
        source_in_bias,
        source_out_taps,
    )


def solution(mesh):
    placed = (P("wide", None, None), P("narrow", "wide", None), P(), P(), P(), P(), P(), P())
    return jax.shard_map(
        on_device,
        mesh=mesh,
        in_specs=placed,
        out_specs=P("narrow", "wide", None, None),
        check_vma=False,
    )
```

```python
import functools

import jax
import jax.numpy as jnp
from jax import lax
from jax.experimental import pallas as pl
from jax.experimental.pallas import tpu as pltpu
from jax.sharding import PartitionSpec as P

F32 = jnp.float32
BF16 = jnp.bfloat16
OFF = -1e38


def split(value):
    high = value.astype(BF16)
    return high, (value - high.astype(F32)).astype(BF16)


def spread_taps(t_in, t_bias, t_out, in_rows, out_rows):
    lane = lax.broadcasted_iota(jnp.int32, (1, 256), 1) & 15
    row = lax.broadcasted_iota(jnp.int32, (16, 128), 0)
    for n in range(10):
        value = jnp.zeros((1, 256), F32)
        for h in range(16):
            value = jnp.where(lane == h, t_in[h, n] if n < 9 else t_bias[h], value)
        in_rows[n : n + 1, :] = value
    for n in range(9):
        value = jnp.zeros((16, 128), F32)
        for h in range(16):
            value = jnp.where(row == h, t_out[h, n], value)
        out_rows[n] = value


def place_of(cell):
    inner = (cell * 171) >> 10
    rest = cell - 84
    l_edge, k_edge = rest >> 2, rest & 3
    l_hid = jnp.where(cell < 84, inner, l_edge)
    k_hid = jnp.where(cell < 84, cell - inner * 6 + 2, jnp.where(k_edge < 2, k_edge, k_edge + 6))
    return l_hid, k_hid


def chosen(code, taps):
    value = jnp.zeros(code.shape, F32)
    for a in range(3):
        for b in range(3):
            value = jnp.where(code == b * 16 + a, taps(3 * a + b), value)
    return value


def build_target_weights(in_taps_ref, out_taps_ref, w1, wh, w2):
    def taps_in(n):
        return in_taps_ref[n : n + 1, :]

    def chunk(c, carry):
        shape = (128, 256)
        row = lax.broadcasted_iota(jnp.int32, shape, 0)
        cell = (lax.broadcasted_iota(jnp.int32, (1, 256), 1) + c * 256) >> 4
        l_hid, k_hid = place_of(cell)
        code = ((row >> 3) - l_hid) * 16 + (((row & 7) - k_hid + 2) & 15)
        lanes = pl.ds(pl.multiple_of(c * 256, 256), 256)
        high, low = split(chosen(code, taps_in))
        w1[0:128, lanes] = high
        w1[128:256, lanes] = low

        cell = lax.broadcasted_iota(jnp.int32, (16, 1, 128), 0) + c * 16
        lane = lax.broadcasted_iota(jnp.int32, (16, 1, 128), 2)
        l_hid, k_hid = place_of(cell)
        code = (l_hid - (lane >> 3)) * 16 + ((k_hid - (lane & 7)) & 15)
        code = jnp.broadcast_to(code, (16, 16, 128))
        high, low = split(chosen(code, lambda n: out_taps_ref[n][None]).reshape(256, 128))
        rows = pl.ds(pl.multiple_of(c * 256, 256), 256)
        w2[rows, 0:128] = high
        w2[rows, 128:256] = low
        return carry

    lax.fori_loop(0, 9, chunk, 0)

    def edge_chunk(c, carry):
        row = lax.broadcasted_iota(jnp.int32, (64, 256), 0)
        cell = (lax.broadcasted_iota(jnp.int32, (1, 256), 1) + c * 256 + 1280) >> 4
        l_hid, k_hid = place_of(cell)
        m = row & 3
        k_in = jnp.where(m < 2, m - 2, m + 6)
        code = ((row >> 2) - l_hid) * 16 + ((k_in - k_hid + 2) & 15)
        lanes = pl.ds(pl.multiple_of(c * 256, 256), 256)
        high, low = split(chosen(code, taps_in))
        wh[0:64, lanes] = high
        wh[64:128, lanes] = low
        return carry

    lax.fori_loop(0, 4, edge_chunk, 0)


def target_bias(block, first, spread_ref, bias):
    shape = (11, 2304)
    patch = lax.broadcasted_iota(jnp.int32, shape, 0) + first
    patch = jnp.where(patch >= 11, patch - 11, patch)
    cell = lax.broadcasted_iota(jnp.int32, (1, 2304), 1) >> 4
    l_hid, k_hid = place_of(cell)
    k_at = k_hid - 1 + block * 8
    l_at = patch * 12 - 1 + l_hid
    valid = (l_at >= 0) & (l_at < 128) & (k_at >= 0) & (k_at < 32) & (cell < 140)
    spread = jnp.concatenate([spread_ref[9:10, :]] * 9, axis=1)
    bias[...] = jnp.where(valid, spread, OFF)


def target_chunk(c, steps, x, xh, bias, w1, wh, w2, acc):
    rows = slice(steps.start * 128, steps.stop * 128)
    count = steps.stop - steps.start
    lanes = slice(c * 256, (c + 1) * 256)
    hidden = jnp.dot(x[rows, :], w1[:, lanes], preferred_element_type=F32)
    if c >= 5:
        edge_lanes = slice(c * 256 - 1280, c * 256 - 1024)
        hidden += jnp.dot(xh[rows, :], wh[:, edge_lanes], preferred_element_type=F32)
    hidden = hidden.reshape(count, 128, 256) + bias[steps, lanes][:, None, :]
    high, low = split(jnp.maximum(hidden, 0.0).reshape(count * 128, 256))
    first = jnp.dot(high, w2[lanes, :], preferred_element_type=F32)
    rest = jnp.dot(low, w2[lanes, 0:128], preferred_element_type=F32)
    if c == 0:
        acc[rows, :] = first
    else:
        acc[rows, :] += first
    acc[rows, 0:128] += rest


def build_source_weights(in_taps, out_taps, w1, w2):
    def band(h, carry):
        shape = (128, 128)
        apart = lax.broadcasted_iota(jnp.int32, shape, 0) - lax.broadcasted_iota(
            jnp.int32, shape, 1
        )
        c, at = h // 2, pl.multiple_of((h % 2) * 128, 128)
        for a in range(3):
            for taps, w, first in ((in_taps, w1, True), (out_taps, w2, False)):
                value = jnp.zeros(shape, F32)
                for b in range(3):
                    value = jnp.where(apart == b - 1, taps[h, 3 * a + b], value)
                for n, part in enumerate(split(value)):
                    other = slice((3 * n + a) * 128, (3 * n + a + 1) * 128)
                    if first:
                        w[c, other, pl.ds(at, 128)] = part
                    else:
                        w[c, pl.ds(at, 128), other] = part
        return carry

    lax.fori_loop(0, 16, band, 0)


def source_section(r_ref, in_bias, out_ref, w1, w2, acc, turned):
    lane = lax.broadcasted_iota(jnp.int32, (1, 256), 1)

    def chunk(c, first, count):
        near = [r_ref[first + a : first + a + count].reshape(count * 16, 128) for a in range(3)]
        rows = slice(first * 16, (first + count) * 16)
        spread = jnp.where(lane < 128, in_bias[2 * c], in_bias[2 * c + 1])
        hidden = jnp.dot(
            jnp.concatenate(near + near, axis=1), w1[c], preferred_element_type=F32
        )
        high, low = split(jnp.maximum(hidden + spread, 0.0))
        both = jnp.dot(high, w2[c], preferred_element_type=F32)
        rest = jnp.dot(low, w2[c, :, 0:384], preferred_element_type=F32)
        total = both[:, 0:384] + both[:, 384:768] + rest
        acc[rows, :] = total if c == 0 else acc[rows, :] + total

    def finish(rows):
        for i in rows:
            total = acc[i * 16 : i * 16 + 16, 128:256]
            if i > 0:
                total += acc[i * 16 - 16 : i * 16, 0:128]
            if i < 63:
                total += acc[i * 16 + 16 : i * 16 + 32, 256:384]
            out_ref[i] = jnp.maximum(total, 0.0).astype(BF16)

    for c in range(7):
        chunk(c, 0, 64)
    chunk(7, 0, 32)
    finish(range(0, 31))
    chunk(7, 32, 32)
    finish(range(31, 64))


MESH = pl.DeviceIdType.MESH


def push(src, dst, send_sem, recv_sem, device):
    return pltpu.make_async_remote_copy(
        src_ref=src,
        dst_ref=dst,
        send_sem=send_sem,
        recv_sem=recv_sem,
        device_id=device,
        device_id_type=MESH,
    )


class Gather:
    def __init__(self, held, send, recv):
        me = lax.axis_index("wide")
        self.narrow = lax.axis_index("narrow")
        self.held, self.send, self.recv = held, send, recv
        self.core = me % 2
        self.at = (me // 16, (me // 2) % 4)
        self.z = (me // 8) % 2
        self.count = 0
        self.copies = []

    def device(self, x=None, y=None, z=None, core=None, narrow=None):
        x = self.at[0] if x is None else x
        y = self.at[1] if y is None else y
        z = self.z if z is None else z
        core = self.core if core is None else core
        narrow = self.narrow if narrow is None else narrow
        return (((x * 2 + z) * 4 + y) * 2 + core, narrow)

    def along(self, half, d, other=0):
        n = (self.at[half] + d) % 4
        return self.device(z=(self.z + other) % 2, **{"xy"[half]: n})

    def partners(self):
        found = [self.device(core=1 - self.core)]
        for d, other in self.near():
            for half in range(2):
                if d > 0 or half == 0:
                    found.append(self.along(half, d, other))
        for step in (1, 3):
            for core in (self.core, 1 - self.core):
                found.append(self.device(core=core, narrow=(self.narrow + step) % 4))
        return found

    def near(self):
        return [(0, 1)] + [(d, other) for other in (0, 1) for d in (1, 3, 2)]

    def start(self, src, arrives, device):
        n = self.count
        self.count += 1
        copy = push(src, src, self.send.at[n], self.recv.at[n], device)
        copy.start()
        self.copies.append(copy)
        return push(src, arrives, self.send.at[n], self.recv.at[n], device)

    def back(self, half, steps):
        at = list(self.at)
        at[half] = (at[half] + 4 - steps) % 4
        return at

    def first(self):
        self.early, self.late = {}, {}
        for d, other in self.near():
            for half in range(2):
                lanes = slice(half * 512, half * 512 + 512)
                x, y = self.at
                src = self.held.at[x, self.z, y, :, lanes]
                x, y = self.back(half, d)
                landed = self.held.at[x, (self.z + other) % 2, y, :, lanes]
                self.early[half, d, other] = self.start(
                    src, landed, self.along(half, d, other)
                )

    def second(self):
        for e in (0, 1, 3, 2):
            for half in range(2):
                lanes = slice(half * 512, half * 512 + 512)
                for other in range(2):
                    if (e, other) != (0, 0):
                        self.early[half, e, other].wait_recv()
                at = self.back(half, e)
                x, y = at
                src = self.held.at[x, :, y, :, lanes]
                for d in (1, 3, 2):
                    x, y = at
                    if half == 0:
                        y = (y + 4 - d) % 4
                    else:
                        x = (x + 4 - d) % 4
                    landed = self.held.at[x, :, y, :, lanes]
                    self.late[half, e, d] = self.start(
                        src, landed, self.along(1 - half, d)
                    )

    def finish(self):
        for landed in self.late.values():
            landed.wait_recv()
        for copy in self.copies:
            copy.wait_send()


def whole_kernel(
    t_given,
    s_given,
    t_in_given,
    t_bias_given,
    t_out_given,
    s_in_given,
    s_bias_given,
    s_out_given,
    out_ref,
    t_ref,
    t_in,
    t_bias,
    t_out,
    s_in,
    s_bias,
    s_out,
    given_sem,
    held,
    x_t,
    xh_t,
    w1,
    wh,
    w2,
    x,
    xh,
    bias,
    acc,
    s_all,
    cells_f,
    cells_out,
    cells_in,
    edge,
    edge_in,
    section,
    received,
    w3,
    w4,
    acc4,
    turned,
    in_rows,
    out_rows,
    g_send,
    g_recv,
    e_send,
    e_recv,
    a_send,
    a_recv,
):
    me = lax.axis_index("wide")
    block = lax.axis_index("narrow")
    gather = Gather(held, g_send, g_recv)
    core = gather.core
    barrier = pltpu.get_barrier_semaphore()
    partners = gather.partners()
    for partner in partners:
        pl.semaphore_signal(barrier, inc=1, device_id=partner, device_id_type=MESH)
    loads = [
        pltpu.make_async_copy(src, dst, given_sem.at[n])
        for n, (src, dst) in enumerate(
            (
                (t_given, t_ref),
                (s_given, s_all.at[0:128]),
                (t_in_given, t_in),
                (t_bias_given, t_bias),
                (t_out_given, t_out),
                (s_in_given, s_in),
                (s_bias_given, s_bias),
                (s_out_given, s_out),
            )
        )
    ]
    for load in loads:
        load.start()
    x_t[...] = jnp.zeros_like(x_t)
    xh_t[...] = jnp.zeros_like(xh_t)
    for n in (0, 65):
        received[n] = jnp.zeros((16, 128), BF16)
    loads[0].wait()
    mine = t_ref[...].astype(F32)
    mine = jnp.concatenate([mine[:, 0, :], mine[:, 1, :]], axis=0)
    held[gather.at[0], gather.z, gather.at[1]] = mine.astype(BF16)
    for load in loads[1:]:
        load.wait()
    pl.semaphore_wait(barrier, len(partners))

    sibling = gather.device(core=1 - core)
    gather.first()
    other_row = push(s_all.at[0:128], s_all.at[128:256], e_send.at[5], e_recv.at[5], sibling)
    other_row.start()
    spread_taps(t_in, t_bias, t_out, in_rows, out_rows)
    build_target_weights(in_rows, out_rows, w1, wh, w2)
    target_bias(block, me // 6, in_rows, bias)
    gather.second()
    build_source_weights(s_in, s_out, w3, w4)
    other_row.wait()
    gather.finish()

    scale = s_all.shape[-1] ** (-0.5)
    product = lax.dot_general(
        held[...].reshape(512, 1024),
        s_all[...],
        (((1,), (1,)), ((), ())),
        preferred_element_type=F32,
    )
    product = (product * scale).astype(BF16)
    cells_f[0] = product[:, 0:128].astype(F32)
    cells_f[1] = product[:, 128:256].astype(F32)
    cells_out[...] = product[:, 128:256]
    copies = []
    n = 4
    copies.append(push(cells_out, cells_in, e_send.at[n], e_recv.at[n], sibling))
    copies[0].start()
    for up, slots in enumerate(((0, 1), (6, 7))):
        for away in range(2):
            n = up * 2 + away
            for m, slot in enumerate(slots):
                rows = cells_f[away, pl.ds(slot, 64, stride=8), :]
                edge[n, m * 64 : (m + 1) * 64, :] = rows.astype(BF16)
            device = gather.device(
                core=(core + away) % 2, narrow=(block + (1 if up else 3)) % 4
            )
            copy = push(edge.at[n], edge_in.at[n], e_send.at[n], e_recv.at[n], device)
            copy.start()
            copies.append(copy)

    def place(cells, core):
        for n in range(64):
            first = pl.multiple_of(16 + core * 16 + (n // 2) * 32 + (n % 2) * 8, 8)
            x_t[pl.ds(first, 8), :] = cells[n * 8 : n * 8 + 8]

    patches = [(me // 6 + step) % 11 for step in range(11)]
    place(cells_f[0], core)
    copies[0].wait()
    place(cells_in[...].astype(F32), 1 - core)
    for step, p in enumerate(patches):
        turned_part = x_t[pl.ds(pl.multiple_of(p * 96, 32), 128), :].T.astype(BF16)
        x[step * 128 : step * 128 + 128, 0:128] = turned_part
        x[step * 128 : step * 128 + 128, 128:256] = turned_part

    every = slice(0, 11)
    for c in range(5):
        target_chunk(c, every, x, xh, bias, w1, wh, w2, acc)

    for copy in copies[1:]:
        copy.wait()
    for up, (inside, slots) in enumerate(((block < 3, (2, 3)), (block > 0, (0, 1)))):
        for away in range(2):
            at = (core + away) % 2
            for m, slot in enumerate(slots):
                value = edge_in[up * 2 + away, m * 64 : (m + 1) * 64, :].astype(F32)
                value = jnp.where(inside, value, 0.0)
                cells_f[away, 0:64, :] = value
                for l in range(2):
                    xh_t[pl.ds(8 + at * 8 + l * 4 + slot, 32, stride=16), :] = cells_f[
                        away, pl.ds(l, 32, stride=2), :
                    ]
    for step, p in enumerate(patches):
        turned_part = xh_t[pl.ds(pl.multiple_of(p * 48, 16), 64), :].T.astype(BF16)
        xh[step * 128 : step * 128 + 128, :] = jnp.concatenate(
            [turned_part, turned_part], axis=1
        )

    for steps in (slice(0, 6), slice(6, 11)):
        for c in range(5, 9):
            target_chunk(c, steps, x, xh, bias, w1, wh, w2, acc)
        for step in range(steps.start, steps.stop):
            p = patches[step]
            rows = slice(step * 128, step * 128 + 128)
            total = jnp.maximum(acc[rows, 0:128] + acc[rows, 128:256], 0.0).T
            section[pl.ds(pl.multiple_of(p * 96, 32), 96), :] = total[:96].astype(BF16)
        for step in range(steps.start, steps.stop):
            for q in range(6):
                to = patches[step] * 6 + q

                @pl.when((to < 64) & (to != me))
                def _():
                    src = section.at[pl.ds(pl.multiple_of(to * 16, 16), 16)]
                    push(src, received.at[me + 1], a_send, a_recv, (to, block)).start()

    received[me + 1] = section[pl.ds(pl.multiple_of(me * 16, 16), 16)]
    everything = pltpu.make_async_copy(
        received.at[0:63], received.at[0:63], a_recv
    )
    everything.wait()
    source_section(received, s_bias, out_ref, w3, w4, acc4, turned)
    pltpu.make_async_copy(section.at[0:1008], section.at[0:1008], a_send).wait()


VMEM = pl.BlockSpec(memory_space=pltpu.VMEM)


def on_device(
    source_features,
    target_features,
    target_in_taps,
    target_in_bias,
    target_out_taps,
    source_in_taps,
    source_in_bias,
    source_out_taps,
):
    result = pl.pallas_call(
        whole_kernel,
        out_shape=pltpu.VMEM((64, 16, 128), BF16),
        in_specs=[pl.BlockSpec(memory_space=pl.ANY)] * 8,
        out_specs=VMEM,
        scratch_shapes=[
            pltpu.VMEM((8, 2, 1024), BF16),
            pltpu.SMEM((16, 9), F32),
            pltpu.SMEM((16,), F32),
            pltpu.SMEM((16, 9), F32),
            pltpu.SMEM((16, 9), F32),
            pltpu.SMEM((16,), F32),
            pltpu.SMEM((16, 9), F32),
            pltpu.SemaphoreType.DMA((8,)),
            pltpu.VMEM((4, 2, 4, 16, 1024), BF16),
            pltpu.VMEM((136 * 8, 128), F32),
            pltpu.VMEM((136 * 4, 128), F32),
            pltpu.VMEM((256, 2304), BF16),
            pltpu.VMEM((128, 1024), BF16),
            pltpu.VMEM((2304, 256), BF16),
            pltpu.VMEM((1408, 256), BF16),
            pltpu.VMEM((1408, 128), BF16),
            pltpu.VMEM((11, 2304), F32),
            pltpu.VMEM((1408, 256), F32),
            pltpu.VMEM((256, 1024), BF16),
            pltpu.VMEM((2, 512, 128), F32),
            pltpu.VMEM((512, 128), BF16),
            pltpu.VMEM((512, 128), BF16),
            pltpu.VMEM((4, 128, 128), BF16),
            pltpu.VMEM((4, 128, 128), BF16),
            pltpu.VMEM((1056, 128), BF16),
            pltpu.VMEM((66, 16, 128), BF16),
            pltpu.VMEM((8, 768, 256), BF16),
            pltpu.VMEM((8, 256, 768), BF16),
            pltpu.VMEM((1024, 384), F32),
            pltpu.VMEM((1024, 128), F32),
            pltpu.VMEM((16, 256), F32),
            pltpu.VMEM((9, 16, 128), F32),
            pltpu.SemaphoreType.DMA((38,)),
            pltpu.SemaphoreType.DMA((38,)),
            pltpu.SemaphoreType.DMA((6,)),
            pltpu.SemaphoreType.DMA((6,)),
            pltpu.SemaphoreType.DMA,
            pltpu.SemaphoreType.DMA,
        ],
        compiler_params=pltpu.CompilerParams(
            collective_id=0, has_side_effects=True, vmem_limit_bytes=56 * 2**20
        ),
    )(
        target_features,
        source_features[0],
        target_in_taps,
        target_in_bias,
        target_out_taps,
        source_in_taps,
        source_in_bias,
        source_out_taps,
    )
    return jnp.transpose(result.reshape(64, 2, 8, 128), (2, 1, 0, 3))


def solution(mesh):
    placed = (P("wide", None, None), P("narrow", "wide", None), P(), P(), P(), P(), P(), P())
    return jax.shard_map(
        on_device,
        mesh=mesh,
        in_specs=placed,
        out_specs=P("narrow", "wide", None, None),
        check_vma=False,
    )
```

```python
import functools

import jax
import jax.numpy as jnp
from jax import lax
from jax.experimental import pallas as pl
from jax.experimental.pallas import tpu as pltpu
from jax.sharding import PartitionSpec as P

F32 = jnp.float32
BF16 = jnp.bfloat16
OFF = -1e38


def split(value):
    high = value.astype(BF16)
    return high, (value - high.astype(F32)).astype(BF16)


def spread_taps(t_in, t_bias, t_out, in_rows, out_rows):
    lane = lax.broadcasted_iota(jnp.int32, (1, 256), 1) & 15
    row = lax.broadcasted_iota(jnp.int32, (16, 128), 0)
    for n in range(10):
        value = jnp.zeros((1, 256), F32)
        for h in range(16):
            value = jnp.where(lane == h, t_in[h, n] if n < 9 else t_bias[h], value)
        in_rows[n : n + 1, :] = value
    for n in range(9):
        value = jnp.zeros((16, 128), F32)
        for h in range(16):
            value = jnp.where(row == h, t_out[h, n], value)
        out_rows[n] = value


def place_of(cell):
    inner = (cell * 171) >> 10
    rest = cell - 84
    l_edge, k_edge = rest >> 2, rest & 3
    l_hid = jnp.where(cell < 84, inner, l_edge)
    k_hid = jnp.where(cell < 84, cell - inner * 6 + 2, jnp.where(k_edge < 2, k_edge, k_edge + 6))
    return l_hid, k_hid


def chosen(code, taps):
    value = jnp.zeros(code.shape, F32)
    for a in range(3):
        for b in range(3):
            value = jnp.where(code == b * 16 + a, taps(3 * a + b), value)
    return value


def build_target_weights(in_taps_ref, out_taps_ref, w1, wh, w2):
    def taps_in(n):
        return in_taps_ref[n : n + 1, :]

    def chunk(c, carry):
        shape = (128, 256)
        row = lax.broadcasted_iota(jnp.int32, shape, 0)
        cell = (lax.broadcasted_iota(jnp.int32, (1, 256), 1) + c * 256) >> 4
        l_hid, k_hid = place_of(cell)
        code = ((row >> 3) - l_hid) * 16 + (((row & 7) - k_hid + 2) & 15)
        lanes = pl.ds(pl.multiple_of(c * 256, 256), 256)
        high, low = split(chosen(code, taps_in))
        w1[0:128, lanes] = high
        w1[128:256, lanes] = low

        cell = lax.broadcasted_iota(jnp.int32, (16, 1, 128), 0) + c * 16
        lane = lax.broadcasted_iota(jnp.int32, (16, 1, 128), 2)
        l_hid, k_hid = place_of(cell)
        code = (l_hid - (lane >> 3)) * 16 + ((k_hid - (lane & 7)) & 15)
        code = jnp.broadcast_to(code, (16, 16, 128))
        high, low = split(chosen(code, lambda n: out_taps_ref[n][None]).reshape(256, 128))
        rows = pl.ds(pl.multiple_of(c * 256, 256), 256)
        w2[rows, 0:128] = high
        w2[rows, 128:256] = low
        return carry

    lax.fori_loop(0, 9, chunk, 0)

    def edge_chunk(c, carry):
        row = lax.broadcasted_iota(jnp.int32, (64, 256), 0)
        cell = (lax.broadcasted_iota(jnp.int32, (1, 256), 1) + c * 256 + 1280) >> 4
        l_hid, k_hid = place_of(cell)
        m = row & 3
        k_in = jnp.where(m < 2, m - 2, m + 6)
        code = ((row >> 2) - l_hid) * 16 + ((k_in - k_hid + 2) & 15)
        lanes = pl.ds(pl.multiple_of(c * 256, 256), 256)
        high, low = split(chosen(code, taps_in))
        wh[0:64, lanes] = high
        wh[64:128, lanes] = low
        return carry

    lax.fori_loop(0, 4, edge_chunk, 0)


def target_bias(block, first, spread_ref, bias):
    shape = (11, 2304)
    patch = lax.broadcasted_iota(jnp.int32, shape, 0) + first
    patch = jnp.where(patch >= 11, patch - 11, patch)
    cell = lax.broadcasted_iota(jnp.int32, (1, 2304), 1) >> 4
    l_hid, k_hid = place_of(cell)
    k_at = k_hid - 1 + block * 8
    l_at = patch * 12 - 1 + l_hid
    valid = (l_at >= 0) & (l_at < 128) & (k_at >= 0) & (k_at < 32) & (cell < 140)
    spread = jnp.concatenate([spread_ref[9:10, :]] * 9, axis=1)
    bias[...] = jnp.where(valid, spread, OFF)


def target_chunk(c, steps, x, xh, bias, w1, wh, w2, acc):
    rows = slice(steps.start * 128, steps.stop * 128)
    count = steps.stop - steps.start
    lanes = slice(c * 256, (c + 1) * 256)
    hidden = jnp.dot(x[rows, :], w1[:, lanes], preferred_element_type=F32)
    if c >= 5:
        edge_lanes = slice(c * 256 - 1280, c * 256 - 1024)
        hidden += jnp.dot(xh[rows, :], wh[:, edge_lanes], preferred_element_type=F32)
    hidden = hidden.reshape(count, 128, 256) + bias[steps, lanes][:, None, :]
    high, low = split(jnp.maximum(hidden, 0.0).reshape(count * 128, 256))
    first = jnp.dot(high, w2[lanes, :], preferred_element_type=F32)
    rest = jnp.dot(low, w2[lanes, 0:128], preferred_element_type=F32)
    if c == 0:
        acc[rows, :] = first
    else:
        acc[rows, :] += first
    acc[rows, 0:128] += rest


def build_source_weights(in_taps, out_taps, w1, w2):
    def band(h, carry):
        shape = (128, 128)
        apart = lax.broadcasted_iota(jnp.int32, shape, 0) - lax.broadcasted_iota(
            jnp.int32, shape, 1
        )
        c, at = h // 2, pl.multiple_of((h % 2) * 128, 128)
        for a in range(3):
            for taps, w, first in ((in_taps, w1, True), (out_taps, w2, False)):
                value = jnp.zeros(shape, F32)
                for b in range(3):
                    value = jnp.where(apart == b - 1, taps[h, 3 * a + b], value)
                for n, part in enumerate(split(value)):
                    other = slice((3 * n + a) * 128, (3 * n + a + 1) * 128)
                    if first:
                        w[c, other, pl.ds(at, 128)] = part
                    else:
                        w[c, pl.ds(at, 128), other] = part
        return carry

    lax.fori_loop(0, 16, band, 0)


def source_section(r_ref, in_bias, out_ref, w1, w2, acc, turned):
    lane = lax.broadcasted_iota(jnp.int32, (1, 256), 1)

    def chunk(c, first, count):
        near = [r_ref[first + a : first + a + count].reshape(count * 16, 128) for a in range(3)]
        rows = slice(first * 16, (first + count) * 16)
        spread = jnp.where(lane < 128, in_bias[2 * c], in_bias[2 * c + 1])
        hidden = jnp.dot(
            jnp.concatenate(near + near, axis=1), w1[c], preferred_element_type=F32
        )
        high, low = split(jnp.maximum(hidden + spread, 0.0))
        both = jnp.dot(high, w2[c], preferred_element_type=F32)
        rest = jnp.dot(low, w2[c, :, 0:384], preferred_element_type=F32)
        total = both[:, 0:384] + both[:, 384:768] + rest
        acc[rows, :] = total if c == 0 else acc[rows, :] + total

    def finish(rows):
        for i in rows:
            total = acc[i * 16 : i * 16 + 16, 128:256]
            if i > 0:
                total += acc[i * 16 - 16 : i * 16, 0:128]
            if i < 63:
                total += acc[i * 16 + 16 : i * 16 + 32, 256:384]
            out_ref[i] = jnp.maximum(total, 0.0).astype(BF16)

    for c in range(7):
        chunk(c, 0, 64)
    chunk(7, 0, 32)
    finish(range(0, 31))
    chunk(7, 32, 32)
    finish(range(31, 64))


MESH = pl.DeviceIdType.MESH


def push(src, dst, send_sem, recv_sem, device):
    return pltpu.make_async_remote_copy(
        src_ref=src,
        dst_ref=dst,
        send_sem=send_sem,
        recv_sem=recv_sem,
        device_id=device,
        device_id_type=MESH,
    )


class Gather:
    def __init__(self, held, send, recv):
        me = lax.axis_index("wide")
        self.narrow = lax.axis_index("narrow")
        self.held, self.send, self.recv = held, send, recv
        self.core = me % 2
        self.at = (me // 16, (me // 2) % 4)
        self.z = (me // 8) % 2
        self.count = 0
        self.copies = []

    def device(self, x=None, y=None, z=None, core=None, narrow=None):
        x = self.at[0] if x is None else x
        y = self.at[1] if y is None else y
        z = self.z if z is None else z
        core = self.core if core is None else core
        narrow = self.narrow if narrow is None else narrow
        return (((x * 2 + z) * 4 + y) * 2 + core, narrow)

    def along(self, half, d, other=0):
        n = (self.at[half] + d) % 4
        return self.device(z=(self.z + other) % 2, **{"xy"[half]: n})

    def partners(self):
        found = [self.device(core=1 - self.core)]
        for d, other in self.near():
            for half in range(2):
                if d > 0 or half == 0:
                    found.append(self.along(half, d, other))
        for step in (1, 3):
            for core in (self.core, 1 - self.core):
                found.append(self.device(core=core, narrow=(self.narrow + step) % 4))
        return found

    def near(self):
        return [(0, 1)] + [(d, other) for other in (0, 1) for d in (1, 3, 2)]

    def start(self, src, arrives, device):
        n = self.count
        self.count += 1
        copy = push(src, src, self.send.at[n], self.recv.at[n], device)
        copy.start()
        self.copies.append(copy)
        return push(src, arrives, self.send.at[n], self.recv.at[n], device)

    def back(self, half, steps):
        at = list(self.at)
        at[half] = (at[half] + 4 - steps) % 4
        return at

    def first(self):
        self.early, self.late = {}, {}
        for d, other in self.near():
            for half in range(2):
                lanes = slice(half * 512, half * 512 + 512)
                x, y = self.at
                src = self.held.at[x, self.z, y, :, lanes]
                x, y = self.back(half, d)
                landed = self.held.at[x, (self.z + other) % 2, y, :, lanes]
                self.early[half, d, other] = self.start(
                    src, landed, self.along(half, d, other)
                )

    def second(self):
        for e in (0, 1, 3, 2):
            for half in range(2):
                lanes = slice(half * 512, half * 512 + 512)
                for other in range(2):
                    if (e, other) != (0, 0):
                        self.early[half, e, other].wait_recv()
                at = self.back(half, e)
                x, y = at
                src = self.held.at[x, :, y, :, lanes]
                for d in (1, 3, 2):
                    x, y = at
                    if half == 0:
                        y = (y + 4 - d) % 4
                    else:
                        x = (x + 4 - d) % 4
                    landed = self.held.at[x, :, y, :, lanes]
                    self.late[half, e, d] = self.start(
                        src, landed, self.along(1 - half, d)
                    )

    def finish(self):
        for landed in self.late.values():
            landed.wait_recv()
        for copy in self.copies:
            copy.wait_send()


def whole_kernel(
    t_given,
    s_given,
    t_in_given,
    t_bias_given,
    t_out_given,
    s_in_given,
    s_bias_given,
    s_out_given,
    out_ref,
    t_ref,
    t_in,
    t_bias,
    t_out,
    s_in,
    s_bias,
    s_out,
    given_sem,
    held,
    x_t,
    xh_t,
    w1,
    wh,
    w2,
    x,
    xh,
    bias,
    acc,
    s_all,
    cells_f,
    cells_out,
    cells_in,
    edge,
    edge_in,
    section,
    received,
    w3,
    w4,
    acc4,
    turned,
    in_rows,
    out_rows,
    g_send,
    g_recv,
    e_send,
    e_recv,
    a_send,
    a_recv,
):
    me = lax.axis_index("wide")
    block = lax.axis_index("narrow")
    gather = Gather(held, g_send, g_recv)
    core = gather.core
    barrier = pltpu.get_barrier_semaphore()
    partners = gather.partners()
    for partner in partners:
        pl.semaphore_signal(barrier, inc=1, device_id=partner, device_id_type=MESH)
    loads = [
        pltpu.make_async_copy(src, dst, given_sem.at[n])
        for n, (src, dst) in enumerate(
            (
                (t_given, t_ref),
                (s_given, s_all.at[0:128]),
                (t_in_given, t_in),
                (t_bias_given, t_bias),
                (t_out_given, t_out),
                (s_in_given, s_in),
                (s_bias_given, s_bias),
                (s_out_given, s_out),
            )
        )
    ]
    for load in loads:
        load.start()
    x_t[...] = jnp.zeros_like(x_t)
    xh_t[...] = jnp.zeros_like(xh_t)
    for n in (0, 65):
        received[n] = jnp.zeros((16, 128), BF16)
    loads[0].wait()
    mine = t_ref[...].astype(F32)
    mine = jnp.concatenate([mine[:, 0, :], mine[:, 1, :]], axis=0)
    held[gather.at[0], gather.z, gather.at[1]] = mine.astype(BF16)
    for load in loads[1:]:
        load.wait()
    pl.semaphore_wait(barrier, len(partners))

    sibling = gather.device(core=1 - core)
    gather.first()
    other_row = push(s_all.at[0:128], s_all.at[128:256], e_send.at[5], e_recv.at[5], sibling)
    other_row.start()
    spread_taps(t_in, t_bias, t_out, in_rows, out_rows)
    build_target_weights(in_rows, out_rows, w1, wh, w2)
    target_bias(block, me // 6, in_rows, bias)
    gather.second()
    build_source_weights(s_in, s_out, w3, w4)
    other_row.wait()
    gather.finish()

    scale = s_all.shape[-1] ** (-0.5)
    copies = []
    for m in range(2):
        rows = slice(m * 256, m * 256 + 256)
        product = lax.dot_general(
            held[2 * m : 2 * m + 2].reshape(256, 1024),
            s_all[...],
            (((1,), (1,)), ((), ())),
            preferred_element_type=F32,
        )
        product = (product * scale).astype(BF16)
        cells_out[rows, :] = product[:, 128:256]
        n = (4, 6)[m]
        copy = push(
            cells_out.at[rows], cells_in.at[rows], e_send.at[n], e_recv.at[n], sibling
        )
        copy.start()
        copies.append(copy)
        cells_f[0, rows, :] = product[:, 0:128].astype(F32)
        cells_f[1, rows, :] = product[:, 128:256].astype(F32)
    for up, slots in enumerate(((0, 1), (6, 7))):
        for away in range(2):
            n = up * 2 + away
            for m, slot in enumerate(slots):
                rows = cells_f[away, pl.ds(slot, 64, stride=8), :]
                edge[n, m * 64 : (m + 1) * 64, :] = rows.astype(BF16)
            device = gather.device(
                core=(core + away) % 2, narrow=(block + (1 if up else 3)) % 4
            )
            copy = push(edge.at[n], edge_in.at[n], e_send.at[n], e_recv.at[n], device)
            copy.start()
            copies.append(copy)

    def place(cells, core):
        for n in range(64):
            first = pl.multiple_of(16 + core * 16 + (n // 2) * 32 + (n % 2) * 8, 8)
            x_t[pl.ds(first, 8), :] = cells[n * 8 : n * 8 + 8]

    patches = [(me // 6 + step) % 11 for step in range(11)]
    place(cells_f[0], core)
    copies[0].wait()
    copies[1].wait()
    place(cells_in[...].astype(F32), 1 - core)
    for step, p in enumerate(patches):
        turned_part = x_t[pl.ds(pl.multiple_of(p * 96, 32), 128), :].T.astype(BF16)
        x[step * 128 : step * 128 + 128, 0:128] = turned_part
        x[step * 128 : step * 128 + 128, 128:256] = turned_part

    every = slice(0, 11)
    for c in range(5):
        target_chunk(c, every, x, xh, bias, w1, wh, w2, acc)

    for copy in copies[2:]:
        copy.wait()
    for up, (inside, slots) in enumerate(((block < 3, (2, 3)), (block > 0, (0, 1)))):
        for away in range(2):
            at = (core + away) % 2
            for m, slot in enumerate(slots):
                value = edge_in[up * 2 + away, m * 64 : (m + 1) * 64, :].astype(F32)
                value = jnp.where(inside, value, 0.0)
                cells_f[away, 0:64, :] = value
                for l in range(2):
                    xh_t[pl.ds(8 + at * 8 + l * 4 + slot, 32, stride=16), :] = cells_f[
                        away, pl.ds(l, 32, stride=2), :
                    ]
    for step, p in enumerate(patches):
        turned_part = xh_t[pl.ds(pl.multiple_of(p * 48, 16), 64), :].T.astype(BF16)
        xh[step * 128 : step * 128 + 128, :] = jnp.concatenate(
            [turned_part, turned_part], axis=1
        )

    for steps in (slice(0, 6), slice(6, 11)):
        for c in range(5, 9):
            target_chunk(c, steps, x, xh, bias, w1, wh, w2, acc)
        for step in range(steps.start, steps.stop):
            p = patches[step]
            rows = slice(step * 128, step * 128 + 128)
            total = jnp.maximum(acc[rows, 0:128] + acc[rows, 128:256], 0.0).T
            section[pl.ds(pl.multiple_of(p * 96, 32), 96), :] = total[:96].astype(BF16)
        for step in range(steps.start, steps.stop):
            for q in range(6):
                to = patches[step] * 6 + q

                @pl.when((to < 64) & (to != me))
                def _():
                    src = section.at[pl.ds(pl.multiple_of(to * 16, 16), 16)]
                    push(src, received.at[me + 1], a_send, a_recv, (to, block)).start()

    received[me + 1] = section[pl.ds(pl.multiple_of(me * 16, 16), 16)]
    everything = pltpu.make_async_copy(
        received.at[0:63], received.at[0:63], a_recv
    )
    everything.wait()
    source_section(received, s_bias, out_ref, w3, w4, acc4, turned)
    pltpu.make_async_copy(section.at[0:1008], section.at[0:1008], a_send).wait()


VMEM = pl.BlockSpec(memory_space=pltpu.VMEM)


def on_device(
    source_features,
    target_features,
    target_in_taps,
    target_in_bias,
    target_out_taps,
    source_in_taps,
    source_in_bias,
    source_out_taps,
):
    result = pl.pallas_call(
        whole_kernel,
        out_shape=pltpu.VMEM((64, 16, 128), BF16),
        in_specs=[pl.BlockSpec(memory_space=pl.ANY)] * 8,
        out_specs=VMEM,
        scratch_shapes=[
            pltpu.VMEM((8, 2, 1024), BF16),
            pltpu.SMEM((16, 9), F32),
            pltpu.SMEM((16,), F32),
            pltpu.SMEM((16, 9), F32),
            pltpu.SMEM((16, 9), F32),
            pltpu.SMEM((16,), F32),
            pltpu.SMEM((16, 9), F32),
            pltpu.SemaphoreType.DMA((8,)),
            pltpu.VMEM((4, 2, 4, 16, 1024), BF16),
            pltpu.VMEM((136 * 8, 128), F32),
            pltpu.VMEM((136 * 4, 128), F32),
            pltpu.VMEM((256, 2304), BF16),
            pltpu.VMEM((128, 1024), BF16),
            pltpu.VMEM((2304, 256), BF16),
            pltpu.VMEM((1408, 256), BF16),
            pltpu.VMEM((1408, 128), BF16),
            pltpu.VMEM((11, 2304), F32),
            pltpu.VMEM((1408, 256), F32),
            pltpu.VMEM((256, 1024), BF16),
            pltpu.VMEM((2, 512, 128), F32),
            pltpu.VMEM((512, 128), BF16),
            pltpu.VMEM((512, 128), BF16),
            pltpu.VMEM((4, 128, 128), BF16),
            pltpu.VMEM((4, 128, 128), BF16),
            pltpu.VMEM((1056, 128), BF16),
            pltpu.VMEM((66, 16, 128), BF16),
            pltpu.VMEM((8, 768, 256), BF16),
            pltpu.VMEM((8, 256, 768), BF16),
            pltpu.VMEM((1024, 384), F32),
            pltpu.VMEM((1024, 128), F32),
            pltpu.VMEM((16, 256), F32),
            pltpu.VMEM((9, 16, 128), F32),
            pltpu.SemaphoreType.DMA((38,)),
            pltpu.SemaphoreType.DMA((38,)),
            pltpu.SemaphoreType.DMA((7,)),
            pltpu.SemaphoreType.DMA((7,)),
            pltpu.SemaphoreType.DMA,
            pltpu.SemaphoreType.DMA,
        ],
        compiler_params=pltpu.CompilerParams(
            collective_id=0, has_side_effects=True, vmem_limit_bytes=56 * 2**20
        ),
    )(
        target_features,
        source_features[0],
        target_in_taps,
        target_in_bias,
        target_out_taps,
        source_in_taps,
        source_in_bias,
        source_out_taps,
    )
    return jnp.transpose(result.reshape(64, 2, 8, 128), (2, 1, 0, 3))


def solution(mesh):
    placed = (P("wide", None, None), P("narrow", "wide", None), P(), P(), P(), P(), P(), P())
    return jax.shard_map(
        on_device,
        mesh=mesh,
        in_specs=placed,
        out_specs=P("narrow", "wide", None, None),
        check_vma=False,
    )
```
